32 devices in a mesh: groups: 2 (over y), ctx: 4 (over z), fsdp: 2 (over x), sub: 2 (over core).
Axes of the slice: x: 2, y: 2, z: 4, core: 2. Of those that a mesh axis runs over, the one named last changes fastest.
Arguments:
- streams: bfloat16 [3, 2048, 4096], P(None, ('groups', 'ctx', 'sub'), 'fsdp'), parts along dimension 1, may hold values from -6 to 6
- feat_taps: float32 [3, 7, 4096], P(None, None, 'fsdp'), may hold values from -2.4 to 2.4
- long_filter: bfloat16 [128, 4096], P('ctx', 'fsdp'), may hold values from -0.5 to 0.5
- upstream: bfloat16 [2048, 4096], P(('groups', 'ctx', 'sub'), 'fsdp'), parts along dimension 0, may hold values from -6 to 6
- score_dir: float32 [4096], P('fsdp'), may hold values from -21 to 21
- seg_lengths: int32 [16], P('groups'), parts along dimension 0, may hold values from 1 to 512, 1024 in all
- list_ids: int32 [16], P('groups'), parts along dimension 0, may hold values from 0 to 1
Outputs:
- d_streams: bfloat16 [3, 2048, 4096], P(None, ('groups', 'ctx', 'sub'), 'fsdp'), parts along dimension 1
- d_feat: float32 [6, 7, 4096], P('groups', None, 'fsdp'), parts along dimension 0
- d_filter: float32 [256, 4096], P(('groups', 'ctx'), 'fsdp'), parts along dimension 0
The draws below stay inside these ranges and needn't reach their ends.
There are 2 independent parts, one for each index of `groups`. The reference program is written for one: setup_inputs(seed, part) draws one part's arguments, and reference() takes and returns one part's arrays. A program takes and returns all parts, laid end to end along the dimension named above; an argument that names none is the same for every part. Nothing has to cross between parts.
Inputs may be any that keep to these rules, and one draw needn't show every extreme that they name: `seg_lengths`: the lengths sum to 1024 and the longest segment has exactly 512 tokens.
All inputs are finite; a program needn't handle non-finite values.
Results may differ from the reference program's by a relative error of at most 0.012.
Values may be sent and summed in bfloat16 or wider, within the bound.
No kernel may reach another device: no remote copies, remote signals or barrier semaphores. Data moves between devices by JAX's collectives and lax.ppermute only.
A program may use at most 64 MiB of HBM per device.

```python
import math
import jax
import jax.numpy as jnp
import numpy as np
from jax import lax

C = 4096
LH = 128
KF = 7
TOKENS = 1024
SEGS = 8
MOST = 512
LISTS = 2


def with_ends(array, stream_key, smallest, top_value):
    extent = array.shape
    spot = [jax.random.randint(jax.random.fold_in(stream_key, axis), (), 0, extent[axis]) for axis in range(len(extent))]
    array = array.at[tuple(spot)].set(smallest)
    longest = extent.index(max(extent))
    spot[longest] = (spot[longest] + 1) % extent[longest]
    return array.at[tuple(spot)].set(top_value)


def steps_of(key, shape, pieces, smallest, top_value):
    level, own = 1.0, jax.random.fold_in(key, 6)
    for axis_at, blocks in pieces:
        steps = jnp.exp(jax.random.uniform(jax.random.fold_in(own, axis_at), (blocks,), jnp.float32, smallest / len(pieces), top_value / len(pieces)))
        level = level * jnp.repeat(steps, shape[axis_at] // blocks).reshape([-1 if axis == axis_at else 1 for axis in range(len(shape))])
    return level


def profile(count, total, limit, skew):
    portions = [(1 << 20) // math.isqrt(rank ** skew) + 1 for rank in range(2, count + 1)]
    spare, given = total - limit - (count - 1), [1] * (count - 1)
    while spare > 0:
        free = [i for i in range(count - 1) if given[i] < limit]
        pool, budget = sum([portions[i] for i in free]), spare
        for i in free:
            addition = min(limit - given[i], max(1, budget * portions[i] // pool), spare)
            given[i] = given[i] + addition
            spare = spare - addition
    return np.array([limit] + given)


def uneven_parts(own_key, amount, total, reach, lean):
    if amount == 2:
        one = jax.random.randint(own_key, (), max(1, total - reach), min(reach, total - 1) + 1)
        return jnp.stack([one, total - one])
    sizes = jnp.asarray(profile(amount, total, reach, lean), jnp.int32)
    pairs = (amount - 1) // 2
    source_of, taker = sizes[1:1 + 2 * pairs:2], sizes[2:2 + 2 * pairs:2]
    margin = jnp.minimum(source_of - 1, reach - taker)
    shifted = jax.random.randint(jax.random.fold_in(own_key, 1), (pairs,), 0, 1 << 20) % (margin + 1)
    sizes = sizes.at[1:1 + 2 * pairs:2].set(source_of - shifted).at[2:2 + 2 * pairs:2].set(taker + shifted)
    return sizes[jax.random.permutation(jax.random.fold_in(own_key, 2), amount)]


def gaussian(own_key, shape, spread, bound, shards=(), kind=jnp.bfloat16):
    values = jax.random.normal(own_key, shape, jnp.float32) * spread
    if len(shards) > 0:
        values = steps_of(own_key, shape, shards, -0.22, 0.18) * values
    return jnp.clip(values, min=-bound, max=bound).astype(kind)


def setup_inputs(seed: int = 0, part: int = 0) -> dict:
    keys = jax.random.split(jax.random.key(seed), 8)
    own_keys = jax.random.split(jax.random.fold_in(keys[7], part), 8)
    return {
        "streams": gaussian(own_keys[0], (3, TOKENS, C), 1.0, 6.0, ((1, 8), (2, 2))),
        "feat_taps": gaussian(keys[1], (3, KF, C), 0.4, 2.4, ((2, 2),), jnp.float32),
        "long_filter": gaussian(keys[2], (LH, C), LH ** -0.5, 0.5, ((0, 4), (1, 2))),
        "upstream": gaussian(own_keys[3], (TOKENS, C), 1.0, 6.0, ((0, 8), (1, 2))),
        "score_dir": gaussian(keys[4], (C,), 3.5, 21.0, ((0, 2),), jnp.float32),
        "seg_lengths": uneven_parts(own_keys[5], SEGS, TOKENS, MOST, 2).astype(jnp.int32),
        "list_ids": with_ends(jax.random.randint(own_keys[6], (SEGS,), 0, LISTS), jax.random.fold_in(own_keys[6], 1), 0, LISTS - 1).astype(jnp.int32),
    }


HIGH = lax.Precision.HIGHEST


def tap_block(tap_count):
    return 16 if tap_count % 16 == 0 else tap_count


def segment_age(seg_lengths, positions):
    offsets = jnp.cumsum(seg_lengths, dtype=jnp.int32) - seg_lengths
    member = offsets[None, :] <= positions[:, None]
    seg_index = jnp.sum(member.astype(jnp.int32), axis=1, dtype=jnp.int32) - 1
    seg_start = jnp.max(jnp.where(member, offsets[None, :], 0), axis=1)
    return seg_index, (positions - seg_start).astype(jnp.int32)


def causal_taps(tap_table, extended, row_age, tok_rows):
    tap_count = tap_table.shape[0]
    per_turn = tap_block(tap_count)

    def advance(b, running):
        for m in range(per_turn):
            j = b * per_turn + m
            window = lax.dynamic_slice_in_dim(extended, tap_count - 1 - j, tok_rows, 0)
            weight_row = lax.dynamic_index_in_dim(tap_table, j, 0, keepdims=False)
            running = running + jnp.where((row_age >= j)[:, None], weight_row[None, :] * window.astype(jnp.float32), 0.0)
        return running

    start_sum = jnp.zeros((tok_rows, extended.shape[1]), jnp.float32)
    return lax.fori_loop(0, tap_count // per_turn, advance, start_sum)


def reverse_taps(tap_table, extended, ext_age, tok_rows):
    tap_count = tap_table.shape[0]
    per_turn = tap_block(tap_count)

    def advance(b, running):
        for m in range(per_turn):
            j = b * per_turn + m
            window = lax.dynamic_slice_in_dim(extended, j, tok_rows, 0)
            keep = lax.dynamic_slice_in_dim(ext_age, j, tok_rows, 0) >= j
            weight_row = lax.dynamic_index_in_dim(tap_table, j, 0, keepdims=False)
            running = running + jnp.where(keep[:, None], weight_row[None, :] * window.astype(jnp.float32), 0.0)
        return running

    start_sum = jnp.zeros((tok_rows, extended.shape[1]), jnp.float32)
    return lax.fori_loop(0, tap_count // per_turn, advance, start_sum)


def correlate_taps(gradient, extended, row_age, tap_count, tok_rows):
    per_turn = tap_block(tap_count)

    def advance(b, result):
        collected = []
        for m in range(per_turn):
            j = b * per_turn + m
            window = lax.dynamic_slice_in_dim(extended, tap_count - 1 - j, tok_rows, 0)
            product = gradient.astype(jnp.float32) * window.astype(jnp.float32)
            collected.append(jnp.sum(jnp.where((row_age >= j)[:, None], product, 0.0), axis=0))
        return lax.dynamic_update_slice_in_dim(result, jnp.stack(collected), b * per_turn, 0)

    start_rows = jnp.zeros((tap_count, gradient.shape[1]), jnp.float32)
    return lax.fori_loop(0, tap_count // per_turn, advance, start_rows)


def list_coef(totals, seg_lengths, list_ids):
    length_f = seg_lengths.astype(jnp.float32)
    scores = totals / length_f
    mates = (list_ids[:, None] == list_ids[None, :]).astype(jnp.float32)
    mean_score = jnp.dot(mates, scores, precision=HIGH) / jnp.sum(mates, axis=1)
    return (scores - mean_score) / length_f


def reference(streams, feat_taps, long_filter, upstream, score_dir, seg_lengths, list_ids):
    tok_rows = streams.shape[1]
    positions = jnp.arange(tok_rows, dtype=jnp.int32)
    seg_index, row_age = segment_age(seg_lengths, positions)
    age_span = jnp.concatenate([row_age, jnp.zeros((LH - 1,), jnp.int32)])
    front = [jnp.pad(streams[i], ((KF - 1, 0), (0, 0))) for i in range(3)]
    featured = [causal_taps(feat_taps[i], front[i], row_age, tok_rows).astype(jnp.bfloat16) for i in range(3)]
    query, key_feat, value_feat = featured
    product = (key_feat.astype(jnp.float32) * value_feat.astype(jnp.float32)).astype(jnp.bfloat16)
    filt = long_filter.astype(jnp.float32)
    prod_ext = jnp.pad(product, ((LH - 1, 0), (0, 0)))
    mixed = causal_taps(filt, prod_ext, row_age, tok_rows)
    out_y = query.astype(jnp.float32) * mixed
    projected = jnp.dot(out_y, score_dir, precision=HIGH)
    onehot = (seg_index[:, None] == jnp.arange(SEGS, dtype=jnp.int32)[None, :]).astype(jnp.float32)
    totals = jnp.dot(projected, onehot, precision=HIGH)
    coef = list_coef(totals, seg_lengths, list_ids)
    tok_coef = jnp.dot(onehot, coef, precision=HIGH)
    d_out = upstream.astype(jnp.float32) + tok_coef[:, None] * score_dir[None, :]
    d_query = (d_out * mixed).astype(jnp.bfloat16)
    d_mixed = (d_out * query.astype(jnp.float32)).astype(jnp.bfloat16)
    dm_ext = jnp.pad(d_mixed, ((0, LH - 1), (0, 0)))
    d_prod = reverse_taps(filt, dm_ext, age_span, tok_rows)
    d_key = (d_prod * value_feat.astype(jnp.float32)).astype(jnp.bfloat16)
    d_value = (d_prod * key_feat.astype(jnp.float32)).astype(jnp.bfloat16)
    d_filter = correlate_taps(d_mixed, prod_ext, row_age, LH, tok_rows)
    grads = [d_query, d_key, d_value]
    d_streams = []
    d_feat = []
    for i in range(3):
        grad_ext = jnp.pad(grads[i], ((0, KF - 1), (0, 0)))
        d_streams.append(reverse_taps(feat_taps[i], grad_ext, age_span, tok_rows).astype(jnp.bfloat16))
        d_feat.append(correlate_taps(grads[i], front[i], row_age, KF, tok_rows))
    return jnp.stack(d_streams), jnp.stack(d_feat), d_filter
```

```python
import jax
import jax.numpy as jnp
import numpy as np
from jax import lax
from jax.experimental import pallas as pl
from jax.experimental.pallas import tpu as pltpu
from jax.sharding import PartitionSpec as P

LH = 128
KF = 7
RIM = 16
BF = jnp.bfloat16
F32 = jnp.float32
VMEM_LIMIT = 48 * 1024 * 1024


def passed_along(value, axis, steps):
    count = lax.axis_size(axis)
    leading, last = (max(0, -steps), min(count, count - steps))
    return lax.ppermute(value, axis, [(source, source + steps) for source in range(leading, last)])


def swapped(value, axis, distance):
    count = lax.axis_size(axis)
    return lax.ppermute(value, axis, [(source, source ^ distance) for source in range(count)])


def rotated(value, axis, distance):
    count = lax.axis_size(axis)
    return lax.ppermute(value, axis, [(source, (source + distance) % count) for source in range(count)])


def summed_everywhere(value):
    for axis in ("sub", "fsdp", "ctx"):
        distance = 1
        while distance < lax.axis_size(axis):
            value = value + swapped(value, axis, distance)
            distance *= 2
    return value


def half_wave(rows):
    odd = 2 * np.arange(rows)[:, None] + 1
    span = np.arange(-rows, 2 * rows)[None, :]
    angle = np.pi * ((odd * span) % (4 * rows)) / (2 * rows)
    table = np.concatenate([np.cos(angle), -np.sin(angle)], axis=0)
    before, own, after = np.split(table, 3, axis=1)
    back = own.T / rows
    as_f32 = lambda parts: np.concatenate(parts, axis=1).astype(np.float32)
    return as_f32([own, after]), as_f32([own, before]), as_f32([own]), as_f32([back])


def dot(left, right):
    return jnp.dot(left, right, preferred_element_type=F32)


class Layout:
    def __init__(self, len_ref, rows, tokens):
        self.rows, self.tokens = rows, tokens
        self.count = len_ref.shape[0]
        self.base = (lax.axis_index("ctx") * lax.axis_size("sub") + lax.axis_index("sub")) * rows
        offset = jnp.int32(0)
        self.offsets = []
        for s in range(self.count):
            self.offsets.append(offset)
            offset = offset + len_ref[s]

    def segment(self, position):
        seg = jnp.zeros_like(position)
        for s in range(1, self.count):
            seg = seg + jnp.where(position >= self.offsets[s], 1, 0)
        return jnp.where((position >= 0) & (position < self.tokens), seg, -1)

    def age(self, position):
        start = jnp.zeros_like(position)
        for s in range(1, self.count):
            start = jnp.where(position >= self.offsets[s], self.offsets[s], start)
        return position - start

    def scalar_segment(self, position):
        seg = jnp.int32(0)
        for s in range(1, self.count):
            seg = seg + jnp.where(position >= self.offsets[s], 1, 0)
        return seg

    def span(self):
        return self.scalar_segment(self.base), self.scalar_segment(self.base + self.rows - 1) + 1


def causal_shifts(sm_ref, layout, first):
    rows = layout.rows
    row = lax.broadcasted_iota(jnp.int32, (rows, rows + RIM), 0)
    col = lax.broadcasted_iota(jnp.int32, (rows, rows + RIM), 1)
    age = layout.age(layout.base + first + row)
    for j in range(KF):
        hit = (col == row + (RIM - j)) & (age >= j)
        sm_ref[j * rows : (j + 1) * rows, :] = jnp.where(hit, 1.0, 0.0).astype(BF)


def reverse_shifts(sm_ref, layout):
    rows = layout.rows
    row = lax.broadcasted_iota(jnp.int32, (rows, rows + RIM), 0)
    col = lax.broadcasted_iota(jnp.int32, (rows, rows + RIM), 1)
    age = layout.age(layout.base + col)
    for j in range(KF):
        hit = (col == row + j) & (age >= j)
        sm_ref[j * rows : (j + 1) * rows, :] = jnp.where(hit, 1.0, 0.0).astype(BF)


def tap_sum(sm_ref, taps, x, rows):
    total = None
    for j in range(KF):
        term = dot(sm_ref[j * rows : (j + 1) * rows, :], x) * taps[j : j + 1, :]
        total = term if total is None else total + term
    return total


def feat_kernel(tokens, len_ref, s_ref, halo_ref, taps_ref, q_ref, k_ref, v_ref, z_ref, sm_ref):
    rows = s_ref.shape[1]

    @pl.when(pl.program_id(0) == 0)
    def _():
        causal_shifts(sm_ref, Layout(len_ref, rows, tokens), 0)

    feats = []
    for i, out in enumerate((q_ref, k_ref, v_ref)):
        x = jnp.concatenate([halo_ref[i], s_ref[i]], axis=0)
        feat = tap_sum(sm_ref, taps_ref[i], x, rows).astype(BF)
        out[...] = feat
        feats.append(feat)
    z_ref[...] = (feats[1].astype(F32) * feats[2].astype(F32)).astype(BF)


def segment_columns(ref, layout, first_own, first_rim):
    rows = layout.rows
    col = lax.broadcasted_iota(jnp.int32, ref.shape, 1)
    position = layout.base + jnp.where(col < rows, col + first_own, col - rows + first_rim)
    ref[...] = layout.segment(position).astype(F32)


def segment_rows(ref, layout):
    row = lax.broadcasted_iota(jnp.int32, ref.shape, 0)
    ref[...] = layout.segment(layout.base + row).astype(F32)


def kept(table, seg_table, s):
    return jnp.where(seg_table == s.astype(F32), table, 0.0).astype(BF)


def times(a, b, rows):
    ar, ai, br, bi = a[:rows], a[rows:], b[:rows], b[rows:]
    return jnp.concatenate([ar * br - ai * bi, ar * bi + ai * br], axis=0)


def conj_times(a, b, rows):
    ar, ai, br, bi = a[:rows], a[rows:], b[:rows], b[rows:]
    return jnp.concatenate([ar * br + ai * bi, ar * bi - ai * br], axis=0)


def dzq_kernel(tokens, len_ref, tail_ref, sqn_ref, taps_ref, mine_ref, other_ref, q_ref, z_ref, dir_ref,
               ahead_ref, own_ref, back_ref,
               dzq_ref, qn_ref, h_ref, part_ref, sm_ref, segc_ref, segr_ref, filt_ref):
    rows = q_ref.shape[0]
    layout = Layout(len_ref, rows, tokens)
    step = pl.program_id(0)

    @pl.when(step == 0)
    def _():
        causal_shifts(sm_ref, layout, rows)
        segment_columns(segc_ref, layout, 0, rows)
        segment_rows(segr_ref, layout)
        part_ref[...] = jnp.zeros_like(part_ref)

    x = jnp.concatenate([tail_ref[0], sqn_ref[...]], axis=0)
    qn = tap_sum(sm_ref, taps_ref[0], x, rows).astype(BF)
    qn_ref[...] = qn
    shards, shard = mine_ref.shape[0], mine_ref.shape[1]
    half = jnp.where(step < pl.num_programs(0) // 2, 0, 1)
    here = half == lax.axis_index("sub")
    for d in range(shards):
        at = lax.rem(lax.axis_index("ctx") + (shards - d), shards) * shard
        filt_ref[pl.ds(pl.multiple_of(at, 8), shard), :] = jnp.where(here, mine_ref[d].astype(F32), other_ref[d].astype(F32))
    h = dot(own_ref[...].astype(BF), filt_ref[...].astype(BF))
    h_ref[...] = h
    q_ext = jnp.concatenate([q_ref[...], qn], axis=0)
    dzq_ref[...] = jnp.zeros_like(dzq_ref)
    first, end = layout.span()

    def one_segment(s, carry):
        spectrum = dot(kept(ahead_ref[...], segc_ref[...], s), q_ext)
        g = conj_times(h_ref[...], spectrum, rows).astype(BF)
        term = dot(kept(back_ref[...], segr_ref[...], s), g)
        dzq_ref[...] += term
        prod = term * z_ref[...].astype(F32) * dir_ref[...]
        row = jnp.sum(prod, axis=0, keepdims=True)
        lanes = row[:, :128]
        for c in range(128, row.shape[1], 128):
            lanes = lanes + row[:, c : c + 128]
        part_ref[pl.ds(s, 1), :] += lanes
        return carry

    lax.fori_loop(first, end, one_segment, 0)


def w_kernel(tokens, len_ref, z_ref, zp_ref, h_ref, behind_ref, back_ref, w_ref, segc_ref, segr_ref):
    rows = z_ref.shape[0]
    layout = Layout(len_ref, rows, tokens)

    @pl.when(pl.program_id(0) == 0)
    def _():
        segment_columns(segc_ref, layout, 0, -rows)
        segment_rows(segr_ref, layout)

    z_ext = jnp.concatenate([z_ref[...], zp_ref[...]], axis=0)
    w_ref[...] = jnp.zeros_like(w_ref)
    first, end = layout.span()

    def one_segment(s, carry):
        spectrum = dot(kept(behind_ref[...], segc_ref[...], s), z_ext)
        g = times(h_ref[...], spectrum, rows).astype(BF)
        w_ref[...] += dot(kept(back_ref[...], segr_ref[...], s), g)
        return carry

    lax.fori_loop(first, end, one_segment, 0)


def dzu_kernel(tokens, len_ref, q_ref, qn_ref, up_ref, upn_ref, h_ref, ahead_ref, back_ref, dzu_ref, segc_ref, segr_ref):
    rows = q_ref.shape[0]
    layout = Layout(len_ref, rows, tokens)

    @pl.when(pl.program_id(0) == 0)
    def _():
        segment_columns(segc_ref, layout, 0, rows)
        segment_rows(segr_ref, layout)

    own = (q_ref[...].astype(F32) * up_ref[...].astype(F32)).astype(BF)
    rim = (qn_ref[...].astype(F32) * upn_ref[...].astype(F32)).astype(BF)
    u_ext = jnp.concatenate([own, rim], axis=0)
    dzu_ref[...] = jnp.zeros_like(dzu_ref)
    first, end = layout.span()

    def one_segment(s, carry):
        spectrum = dot(kept(ahead_ref[...], segc_ref[...], s), u_ext)
        g = conj_times(h_ref[...], spectrum, rows).astype(BF)
        dzu_ref[...] += dot(kept(back_ref[...], segr_ref[...], s), g)
        return carry

    lax.fori_loop(first, end, one_segment, 0)


def coefficients(len_ref, ids_ref, part_ref):
    count = len_ref.shape[0]
    index = lax.broadcasted_iota(jnp.int32, (count, 128), 0)
    length = jnp.zeros((count, 128), F32)
    ids = jnp.zeros((count, 128), jnp.int32)
    for s in range(count):
        length = jnp.where(index == s, len_ref[s].astype(F32), length)
        ids = jnp.where(index == s, ids_ref[s], ids)
    scores = jnp.broadcast_to(jnp.sum(part_ref[...], axis=1, keepdims=True), (count, 128)) / length
    total = jnp.zeros((count, 128), F32)
    mates = jnp.zeros((count, 128), F32)
    for s in range(count):
        same = jnp.where(ids == ids_ref[s], 1.0, 0.0)
        mates = mates + same
        total = total + same * scores[s : s + 1, :]
    return (scores - total / mates) / length


def token_coefficients(coef, seg):
    spread = jnp.zeros(seg.shape, F32)
    for s in range(coef.shape[0]):
        spread = jnp.where(seg == s, coef[s : s + 1, :], spread)
    return spread


def across(column, width):
    return jnp.concatenate([column] * (width // 128), axis=1)


def dfilter_kernel(tokens, sub_ref, len_ref, ids_ref, part_ref, z_ref, q_ref, qn_ref, up_ref, upn_ref, dir_ref,
                   ahead_ref, own_ref, back_ref, send_ref, keep_ref, segc_ref, coef_ref, acc_ref):
    rows, width = z_ref.shape
    layout = Layout(len_ref, rows, tokens)
    step = pl.program_id(0)

    @pl.when(step == 0)
    def _():
        segment_columns(segc_ref, layout, 0, rows)
        coef = coefficients(len_ref, ids_ref, part_ref)
        position = layout.base + lax.broadcasted_iota(jnp.int32, (2 * rows, 128), 0)
        coef_ref[...] = token_coefficients(coef, layout.segment(position))

    parts = []
    for n, (q, up) in enumerate(((q_ref, up_ref), (qn_ref, upn_ref))):
        dy = up[...].astype(F32) + across(coef_ref[n * rows : (n + 1) * rows, :], width) * dir_ref[...]
        parts.append((dy * q[...].astype(F32)).astype(BF))
    dw_ext = jnp.concatenate(parts, axis=0)
    acc_ref[...] = jnp.zeros_like(acc_ref)
    first, end = layout.span()

    def one_segment(s, carry):
        z_spec = dot(kept(own_ref[...], segc_ref[:, :rows], s), z_ref[...])
        spectrum = dot(kept(ahead_ref[...], segc_ref[...], s), dw_ext)
        acc_ref[...] += conj_times(z_spec, spectrum, rows)
        return carry

    lax.fori_loop(first, end, one_segment, 0)
    result = dot(back_ref[...].astype(BF), acc_ref[...].astype(BF))
    half = pl.num_programs(0) // 2

    @pl.when(step < half)
    def _():
        send_ref[...] = result.astype(BF)

    @pl.when(step >= half)
    def _():
        keep_ref[...] = result


def grads_kernel(tokens, sub_ref, len_ref, ids_ref, part_ref, s_ref, halo_ref, q_ref, k_ref, v_ref, up_ref, dir_ref,
                 w_ref, dzu_ref, dzq_ref, da_ref, send_ref, keep_ref, sm_ref, coef_ref):
    rows, width = q_ref.shape
    layout = Layout(len_ref, rows, tokens)
    step = pl.program_id(0)

    @pl.when(step == 0)
    def _():
        causal_shifts(sm_ref, layout, 0)
        coef = coefficients(len_ref, ids_ref, part_ref)
        position = layout.base + lax.broadcasted_iota(jnp.int32, (rows, 128), 0)
        coef_ref[...] = token_coefficients(coef, layout.segment(position))

    rise = across(coef_ref[...], width) * dir_ref[...]
    dz = dzu_ref[...] + rise * dzq_ref[...]
    dq = ((up_ref[...].astype(F32) + rise) * w_ref[...]).astype(BF)
    dk = (dz * v_ref[...].astype(F32)).astype(BF)
    dv = (dz * k_ref[...].astype(F32)).astype(BF)
    blocks = []
    for i, da in enumerate((dq, dk, dv)):
        da_ref[i] = da
        grad = da.astype(F32)
        x = jnp.concatenate([halo_ref[i], s_ref[i]], axis=0)
        sums = []
        for j in range(KF):
            sums.append(jnp.sum(grad * dot(sm_ref[j * rows : (j + 1) * rows, :], x), axis=0, keepdims=True))
        sums.append(jnp.zeros_like(sums[0]))
        blocks.append(jnp.concatenate(sums, axis=0))
    result = jnp.concatenate(blocks, axis=0)
    half = pl.num_programs(0) // 2

    @pl.when(step < half)
    def _():
        send_ref[...] = result

    @pl.when(step >= half)
    def _():
        keep_ref[...] = result


def dstreams_kernel(tokens, len_ref, da_ref, rim_ref, taps_ref, out_ref, sm_ref):
    rows = da_ref.shape[1]

    @pl.when(pl.program_id(0) == 0)
    def _():
        reverse_shifts(sm_ref, Layout(len_ref, rows, tokens))

    for i in range(3):
        x = jnp.concatenate([da_ref[i], rim_ref[i]], axis=0)
        out_ref[i] = tap_sum(sm_ref, taps_ref[i], x, rows).astype(BF)


def shares_kernel(keep_ref, recv_ref, own_ref, *share_refs):
    count = len(share_refs) + 1
    shard = own_ref.shape[0]
    for d in range(count):
        at = pl.ds(pl.multiple_of(lax.rem(lax.axis_index("ctx") + d, count) * shard, 8), shard)
        total = keep_ref[at, :] + recv_ref[at, :].astype(F32)
        if d == 0:
            own_ref[...] = total
        else:
            share_refs[d - 1][...] = total.astype(BF)


def finish_kernel(own_ref, feat_ref, *refs):
    count = (len(refs) - 3) // 2 + 1
    shares, feats = refs[: count - 1], refs[count - 1 : 2 * (count - 1)]
    out_ref, out_feat_ref, slot_ref = refs[2 * (count - 1) :]
    total = own_ref[...]
    for share in shares:
        total = total + share[...].astype(F32)
    out_ref[...] = total
    for d, feat in enumerate((feat_ref, *feats)):
        slot_ref[lax.rem(lax.axis_index("ctx") + (count - d), count)] = feat[...].astype(F32)
    total = slot_ref[0]
    for d in range(1, count):
        total = total + slot_ref[d]
    out_feat_ref[...] = total


def joined_kernel(mine_ref, other_ref, feat_ref, other_feat_ref, dfilt_ref, dfeat_ref):
    width = mine_ref.shape[1]
    here = pl.multiple_of(lax.axis_index("sub") * width, 128)
    there = pl.multiple_of((1 - lax.axis_index("sub")) * width, 128)
    for at, filt, feat in ((here, mine_ref, feat_ref), (there, other_ref, other_feat_ref)):
        dfilt_ref[:, pl.ds(at, width)] = filt[...]
        for i in range(3):
            dfeat_ref[i, :, pl.ds(at, width)] = feat[8 * i : 8 * i + KF, :]


def local(streams, feat_taps, long_filter, upstream, score_dir, seg_lengths, list_ids):
    rows, chans = streams.shape[1:]
    segs = seg_lengths.shape[0]
    shard = long_filter.shape[0]
    ring = ("ctx", "sub")
    tokens = rows * lax.axis_size("ctx") * lax.axis_size("sub")
    shards = lax.axis_size("ctx")
    tile = min(512, chans // 2)
    steps = chans // tile
    half = steps // 2
    ahead, behind, own_wave, back = (jnp.asarray(t) for t in half_wave(rows))
    sub = lax.axis_index("sub")
    sub_of = sub.astype(jnp.int32).reshape(1)
    direction = score_dir.reshape(1, chans)

    smem = pl.BlockSpec(memory_space=pltpu.SMEM)
    blk = lambda *shape: pl.BlockSpec((*shape, tile), lambda i: (0,) * len(shape) + (i,))
    whole = lambda *shape: pl.BlockSpec(shape, lambda i: (0,) * len(shape))
    out = lambda shape, dtype: jax.ShapeDtypeStruct(shape, dtype)
    params = pltpu.CompilerParams(vmem_limit_bytes=VMEM_LIMIT, dimension_semantics=("arbitrary",))
    cost = lambda us: pl.CostEstimate(flops=int(us * 1e9), bytes_accessed=int(us * 3e6), transcendentals=0)

    sq_next = passed_along(streams[0], ring, -1)
    halo = passed_along(streams[:, rows - RIM :, :], ring, 1)
    part = lax.dynamic_slice_in_dim(long_filter, sub * (chans // 2), chans // 2, 1)
    mine = jnp.stack([part] + [rotated(part, "ctx", d) for d in range(1, shards)])
    up_next = passed_along(upstream, ring, -1)
    other = swapped(mine, "sub", 1)

    query, key_feat, value_feat, product = pl.pallas_call(
        lambda *refs: feat_kernel(tokens, *refs),
        grid=(steps,),
        in_specs=[smem, blk(3, rows), blk(3, RIM), blk(3, KF)],
        out_specs=[blk(rows)] * 4,
        out_shape=[out((rows, chans), BF)] * 4,
        scratch_shapes=[pltpu.VMEM((KF * rows, rows + RIM), BF)],
        compiler_params=params, cost_estimate=cost(3), name="feats",
    )(seg_lengths, streams, halo, feat_taps)
    z_prev = passed_along(product, ring, 1)

    half_blk = pl.BlockSpec((shards, shard, tile), lambda i: (0, 0, i % half))
    dzq, q_next, spectrum, partial = pl.pallas_call(
        lambda *refs: dzq_kernel(tokens, *refs),
        grid=(steps,),
        in_specs=[smem, pl.BlockSpec((1, RIM, tile), lambda i: (0, rows // RIM - 1, i)), blk(rows), blk(3, KF),
                  half_blk, half_blk, blk(rows), blk(rows), blk(1),
                  whole(2 * rows, 2 * rows), whole(2 * rows, rows), whole(rows, 2 * rows)],
        out_specs=[blk(rows), blk(rows), blk(2 * rows), whole(segs, 128)],
        out_shape=[out((rows, chans), F32), out((rows, chans), BF), out((2 * rows, chans), F32), out((segs, 128), F32)],
        scratch_shapes=[pltpu.VMEM((KF * rows, rows + RIM), BF), pltpu.VMEM((2 * rows, 2 * rows), F32),
                        pltpu.VMEM((rows, 2 * rows), F32), pltpu.VMEM((LH, tile), F32)],
        compiler_params=params, cost_estimate=cost(3), name="adjoint_of_q",
    )(seg_lengths, streams, sq_next, feat_taps, mine, other, query, product, direction, ahead, own_wave, back)

    totals = summed_everywhere(partial)

    mixed = pl.pallas_call(
        lambda *refs: w_kernel(tokens, *refs),
        grid=(steps,),
        in_specs=[smem, blk(rows), blk(rows), blk(2 * rows), whole(2 * rows, 2 * rows), whole(rows, 2 * rows)],
        out_specs=blk(rows),
        out_shape=out((rows, chans), F32),
        scratch_shapes=[pltpu.VMEM((2 * rows, 2 * rows), F32), pltpu.VMEM((rows, 2 * rows), F32)],
        compiler_params=params, cost_estimate=cost(3), name="mixed",
    )(seg_lengths, product, z_prev, spectrum, behind, back)

    dzu = pl.pallas_call(
        lambda *refs: dzu_kernel(tokens, *refs),
        grid=(steps,),
        in_specs=[smem, blk(rows), blk(rows), blk(rows), blk(rows), blk(2 * rows),
                  whole(2 * rows, 2 * rows), whole(rows, 2 * rows)],
        out_specs=blk(rows),
        out_shape=out((rows, chans), F32),
        scratch_shapes=[pltpu.VMEM((2 * rows, 2 * rows), F32), pltpu.VMEM((rows, 2 * rows), F32)],
        compiler_params=params, cost_estimate=cost(3), name="adjoint_of_up",
    )(seg_lengths, query, q_next, upstream, up_next, spectrum, ahead, back)

    turned = lambda i, ref: lax.rem(i + (1 - ref[0]) * half, steps)
    tblk = lambda *shape: pl.BlockSpec((*shape, tile), lambda i, ref: (0,) * len(shape) + (turned(i, ref),))
    twhole = lambda *shape: pl.BlockSpec(shape, lambda i, ref: (0,) * len(shape))
    tsend = lambda *shape: pl.BlockSpec((*shape, tile), lambda i, ref: (0,) * len(shape) + (jnp.minimum(i, half - 1),))
    tkeep = lambda *shape: pl.BlockSpec((*shape, tile), lambda i, ref: (0,) * len(shape) + (jnp.maximum(i - half, 0),))

    f_send, f_keep = pl.pallas_call(
        lambda *refs: dfilter_kernel(tokens, *refs),
        grid_spec=pltpu.PrefetchScalarGridSpec(
            num_scalar_prefetch=1, grid=(steps,),
            in_specs=[smem, smem, twhole(segs, 128)] + [tblk(rows)] * 5 + [tblk(1)]
            + [twhole(2 * rows, 2 * rows), twhole(2 * rows, rows), twhole(rows, 2 * rows)],
            out_specs=[tsend(LH), tkeep(LH)],
            scratch_shapes=[pltpu.VMEM((2 * rows, 2 * rows), F32), pltpu.VMEM((2 * rows, 128), F32),
                            pltpu.VMEM((2 * rows, tile), F32)],
        ),
        out_shape=[out((LH, chans // 2), BF), out((LH, chans // 2), F32)],
        compiler_params=params, cost_estimate=cost(3), name="filter_grad",
    )(sub_of, seg_lengths, list_ids, totals, product, query, q_next, upstream, up_next, direction, ahead, own_wave, back)
    f_recv = swapped(f_send, "sub", 1)

    grads, t_send, t_keep = pl.pallas_call(
        lambda *refs: grads_kernel(tokens, *refs),
        grid_spec=pltpu.PrefetchScalarGridSpec(
            num_scalar_prefetch=1, grid=(steps,),
            in_specs=[smem, smem, twhole(segs, 128), tblk(3, rows), tblk(3, RIM)] + [tblk(rows)] * 4 + [tblk(1)]
            + [tblk(rows)] * 3,
            out_specs=[tblk(3, rows), tsend(24), tkeep(24)],
            scratch_shapes=[pltpu.VMEM((KF * rows, rows + RIM), BF), pltpu.VMEM((rows, 128), F32)],
        ),
        out_shape=[out((3, rows, chans), BF), out((24, chans // 2), F32), out((24, chans // 2), F32)],
        compiler_params=params, cost_estimate=cost(3), name="input_grads",
    )(sub_of, seg_lengths, list_ids, totals, streams, halo, query, key_feat, value_feat, upstream, direction,
      mixed, dzu, dzq)
    rim = passed_along(grads[:, :RIM, :], ring, -1)

    shares = pl.pallas_call(
        shares_kernel,
        out_shape=[out((shard, chans // 2), F32)] + [out((shard, chans // 2), BF)] * (shards - 1),
        compiler_params=pltpu.CompilerParams(vmem_limit_bytes=VMEM_LIMIT), cost_estimate=cost(1), name="filter_shares",
    )(f_keep, f_recv)
    f_parts = [rotated(shares[d], "ctx", d) for d in range(1, shards)]
    t_sum = (t_keep + swapped(t_send, "sub", 1)).astype(BF)
    t_parts = [rotated(t_sum, "ctx", d) for d in range(1, shards)]

    d_streams = pl.pallas_call(
        lambda *refs: dstreams_kernel(tokens, *refs),
        grid=(steps,),
        in_specs=[smem, blk(3, rows), blk(3, RIM), blk(3, KF)],
        out_specs=blk(3, rows),
        out_shape=out((3, rows, chans), BF),
        scratch_shapes=[pltpu.VMEM((KF * rows, rows + RIM), BF)],
        compiler_params=params, cost_estimate=cost(3), name="stream_grads",
    )(seg_lengths, grads, rim, feat_taps)

    f_half, t_half = pl.pallas_call(
        finish_kernel,
        out_shape=[out((shard, chans // 2), F32), out((24, chans // 2), F32)],
        scratch_shapes=[pltpu.VMEM((shards, 24, chans // 2), F32)],
        compiler_params=pltpu.CompilerParams(vmem_limit_bytes=VMEM_LIMIT), cost_estimate=cost(1), name="shard_sums",
    )(shares[0], t_sum, *f_parts, *t_parts)
    d_filter, d_feat = pl.pallas_call(
        joined_kernel,
        out_shape=[out((shard, chans), F32), out((3, KF, chans), F32)],
        compiler_params=pltpu.CompilerParams(vmem_limit_bytes=VMEM_LIMIT), cost_estimate=cost(1), name="both_halves",
    )(f_half, swapped(f_half, "sub", 1), t_half, swapped(t_half, "sub", 1))
    return (d_streams, d_feat, d_filter)


def solution(mesh):
    placed = (
        P(None, ("groups", "ctx", "sub"), "fsdp"),
        P(None, None, "fsdp"),
        P("ctx", "fsdp"),
        P(("groups", "ctx", "sub"), "fsdp"),
        P("fsdp"),
        P("groups"),
        P("groups"),
    )
    return jax.shard_map(
        local,
        mesh=mesh,
        in_specs=placed,
        out_specs=(
            P(None, ("groups", "ctx", "sub"), "fsdp"),
            P("groups", None, "fsdp"),
            P(("groups", "ctx"), "fsdp"),
        ),
        check_vma=False,
    )
```

```python
import jax
import jax.numpy as jnp
import numpy as np
from jax import lax
from jax.experimental import pallas as pl
from jax.experimental.pallas import tpu as pltpu
from jax.sharding import PartitionSpec as P

LH = 128
KF = 7
RIM = 16
FEAT_ROWS = 24
BF = jnp.bfloat16
F32 = jnp.float32
VMEM_LIMIT = 48 * 1024 * 1024


def passed_along(value, axis, steps):
    count = lax.axis_size(axis)
    leading, last = (max(0, -steps), min(count, count - steps))
    return lax.ppermute(value, axis, [(source, source + steps) for source in range(leading, last)])


def swapped(value, axis, distance):
    count = lax.axis_size(axis)
    return lax.ppermute(value, axis, [(source, source ^ distance) for source in range(count)])


def rotated(value, axis, distance):
    count = lax.axis_size(axis)
    return lax.ppermute(value, axis, [(source, (source + distance) % count) for source in range(count)])


def summed_everywhere(value):
    for axis in ("sub", "fsdp", "ctx"):
        distance = 1
        while distance < lax.axis_size(axis):
            value = value + swapped(value, axis, distance)
            distance *= 2
    return value


def half_wave(rows):
    odd = 2 * np.arange(rows)[:, None] + 1
    span = np.arange(-rows, 2 * rows)[None, :]
    angle = np.pi * ((odd * span) % (4 * rows)) / (2 * rows)
    table = np.concatenate([np.cos(angle), -np.sin(angle)], axis=0)
    before, own, after = np.split(table, 3, axis=1)
    back = own.T / rows
    as_f32 = lambda parts: np.concatenate(parts, axis=1).astype(np.float32)
    return as_f32([own, after]), as_f32([own, before]), as_f32([own]), as_f32([back])


def dot(left, right):
    return jnp.dot(left, right, preferred_element_type=F32)


class Layout:
    def __init__(self, len_ref, rows, tokens):
        self.rows, self.tokens = rows, tokens
        self.count = len_ref.shape[0]
        self.base = (lax.axis_index("ctx") * lax.axis_size("sub") + lax.axis_index("sub")) * rows
        offset = jnp.int32(0)
        self.offsets = []
        for s in range(self.count):
            self.offsets.append(offset)
            offset = offset + len_ref[s]

    def segment(self, position):
        seg = jnp.zeros_like(position)
        for s in range(1, self.count):
            seg = seg + jnp.where(position >= self.offsets[s], 1, 0)
        return jnp.where((position >= 0) & (position < self.tokens), seg, -1)

    def age(self, position):
        start = jnp.zeros_like(position)
        for s in range(1, self.count):
            start = jnp.where(position >= self.offsets[s], self.offsets[s], start)
        return position - start

    def scalar_segment(self, position):
        seg = jnp.int32(0)
        for s in range(1, self.count):
            seg = seg + jnp.where(position >= self.offsets[s], 1, 0)
        return seg

    def span(self):
        return self.scalar_segment(self.base), self.scalar_segment(self.base + self.rows - 1) + 1


def causal_shifts(sm_ref, layout, first):
    rows = layout.rows
    row = lax.broadcasted_iota(jnp.int32, (rows, rows + RIM), 0)
    col = lax.broadcasted_iota(jnp.int32, (rows, rows + RIM), 1)
    age = layout.age(layout.base + first + row)
    for j in range(1, KF):
        hit = (col == row + (RIM - j)) & (age >= j)
        sm_ref[(j - 1) * rows : j * rows, :] = jnp.where(hit, 1.0, 0.0).astype(BF)


def reverse_shifts(sm_ref, layout):
    rows = layout.rows
    row = lax.broadcasted_iota(jnp.int32, (rows, rows + RIM), 0)
    col = lax.broadcasted_iota(jnp.int32, (rows, rows + RIM), 1)
    age = layout.age(layout.base + col)
    for j in range(1, KF):
        hit = (col == row + j) & (age >= j)
        sm_ref[(j - 1) * rows : j * rows, :] = jnp.where(hit, 1.0, 0.0).astype(BF)


def tap_sum(sm_ref, taps, here, x, rows):
    total = here.astype(F32) * taps[0:1, :]
    moved = dot(sm_ref[...], x)
    for j in range(1, KF):
        total = total + moved[(j - 1) * rows : j * rows] * taps[j : j + 1, :]
    return total


def feat_kernel(tokens, len_ref, s_ref, halo_ref, taps_ref, q_ref, k_ref, v_ref, z_ref, sm_ref):
    rows = s_ref.shape[1]

    @pl.when(pl.program_id(0) == 0)
    def _():
        causal_shifts(sm_ref, Layout(len_ref, rows, tokens), 0)

    feats = []
    for i, out in enumerate((q_ref, k_ref, v_ref)):
        x = jnp.concatenate([halo_ref[i], s_ref[i]], axis=0)
        feat = tap_sum(sm_ref, taps_ref[i], s_ref[i], x, rows).astype(BF)
        out[...] = feat
        feats.append(feat)
    z_ref[...] = (feats[1].astype(F32) * feats[2].astype(F32)).astype(BF)


def cut_kernel(streams_ref, filter_ref, query_ref, tail_ref, half_ref, sems):
    rows = streams_ref.shape[1]
    width = half_ref.shape[1]
    at = pl.multiple_of(lax.axis_index("sub") * width, 128)
    copies = [
        pltpu.make_async_copy(streams_ref.at[:, pl.ds(rows - RIM, RIM), :], tail_ref, sems.at[0]),
        pltpu.make_async_copy(filter_ref.at[:, pl.ds(at, width)], half_ref, sems.at[1]),
        pltpu.make_async_copy(streams_ref.at[0], query_ref, sems.at[2]),
    ]
    for copy in copies:
        copy.start()
    for copy in copies:
        copy.wait()


def segment_columns(ref, layout, first_own, first_rim):
    rows = layout.rows
    col = lax.broadcasted_iota(jnp.int32, ref.shape, 1)
    position = layout.base + jnp.where(col < rows, col + first_own, col - rows + first_rim)
    ref[...] = layout.segment(position).astype(F32)


def segment_rows(ref, layout):
    row = lax.broadcasted_iota(jnp.int32, ref.shape, 0)
    ref[...] = layout.segment(layout.base + row).astype(F32)


def kept(table, seg_table, s):
    return jnp.where(seg_table == s.astype(F32), table, 0.0).astype(BF)


def times(a, b, rows):
    ar, ai, br, bi = a[:rows], a[rows:], b[:rows], b[rows:]
    return jnp.concatenate([ar * br - ai * bi, ar * bi + ai * br], axis=0)


def conj_times(a, b, rows):
    ar, ai, br, bi = a[:rows], a[rows:], b[:rows], b[rows:]
    return jnp.concatenate([ar * br + ai * bi, ar * bi - ai * br], axis=0)


def spectra_kernel(tokens, len_ref, z_ref, q_ref, up_ref, own_ref, cross_ref, a_ref, segc_ref, slot_ref, sems):
    rows, width = z_ref.shape
    layout = Layout(len_ref, rows, tokens)
    step = pl.program_id(0)
    last = pl.num_programs(0) - 1

    @pl.when(step == 0)
    def _():
        segment_columns(segc_ref, layout, 0, rows)

    u = (q_ref[...].astype(F32) * up_ref[...].astype(F32)).astype(BF)
    a_ref[...] = jnp.zeros_like(a_ref)
    first, end = layout.span()

    def copy(s, at):
        there = cross_ref.at[s, :, pl.ds(pl.multiple_of(at * width, 128), width)]
        return pltpu.make_async_copy(slot_ref.at[s], there, sems.at[s])

    def one_segment(s, carry):
        wave = kept(own_ref[...], segc_ref[...], s)
        z_spec = dot(wave, z_ref[...])
        cross = conj_times(z_spec, dot(wave, q_ref[...]), rows).astype(BF)

        @pl.when(step > 0)
        def _():
            copy(s, step - 1).wait()

        slot_ref[s] = cross
        copy(s, step).start()
        a_ref[...] += conj_times(z_spec, dot(wave, u), rows)
        return carry

    lax.fori_loop(first, end, one_segment, 0)

    @pl.when(step == last)
    def _():
        def settle(s, carry):
            copy(s, step).wait()
            return carry

        lax.fori_loop(first, end, settle, 0)


def cross_copy(cross_ref, slot_ref, sems, s, at, width):
    here = cross_ref.at[s, :, pl.ds(pl.multiple_of(at * width, 128), width)]
    return pltpu.make_async_copy(here, slot_ref.at[s], sems.at[s])


def score_kernel(tokens, len_ref, tail_ref, sqn_ref, taps_ref, mine_ref, other_ref, z_ref, dir_ref, cross_ref,
                 after_ref, own_ref, qn_ref, h_ref, rim_ref, part_ref, sm_ref, segc_ref, filt_ref, slot_ref, sems):
    rows, width = z_ref.shape
    layout = Layout(len_ref, rows, tokens)
    step = pl.program_id(0)
    first, end = layout.span()

    def fetch(s, carry):
        cross_copy(cross_ref, slot_ref, sems, s, step, width).start()
        return carry

    lax.fori_loop(first, end, fetch, 0)

    @pl.when(step == 0)
    def _():
        causal_shifts(sm_ref, layout, rows)
        segment_columns(segc_ref, layout, 0, rows)
        part_ref[...] = jnp.zeros_like(part_ref)

    x = jnp.concatenate([tail_ref[0], sqn_ref[...]], axis=0)
    qn = tap_sum(sm_ref, taps_ref[0], sqn_ref[...], x, rows).astype(BF)
    qn_ref[...] = qn
    shards, shard = mine_ref.shape[0], mine_ref.shape[1]
    half = jnp.where(step < pl.num_programs(0) // 2, 0, 1)
    here = half == lax.axis_index("sub")
    for d in range(shards):
        at = lax.rem(lax.axis_index("ctx") + (shards - d), shards) * shard
        filt_ref[pl.ds(pl.multiple_of(at, 8), shard), :] = jnp.where(here, mine_ref[d].astype(F32), other_ref[d].astype(F32))
    h_ref[...] = dot(own_ref[...].astype(BF), filt_ref[...].astype(BF))
    z_spec = dot(kept(own_ref[...], segc_ref[:, :rows], end - 1), z_ref[...])
    rim = conj_times(z_spec, dot(kept(after_ref[...], segc_ref[:, rows:], end - 1), qn), rows)
    rim_ref[...] = rim.astype(BF)

    def add(s, cross):
        row = jnp.sum(h_ref[...] * cross, axis=0, keepdims=True) * dir_ref[...] * (1.0 / rows)
        lanes = row[:, :128]
        for c in range(128, row.shape[1], 128):
            lanes = lanes + row[:, c : c + 128]
        part_ref[pl.ds(s, 1), :] += lanes

    add(end - 1, rim)

    def one_segment(s, carry):
        cross_copy(cross_ref, slot_ref, sems, s, step, width).wait()
        add(s, slot_ref[s].astype(F32))
        return carry

    lax.fori_loop(first, end, one_segment, 0)


def dzq_kernel(tokens, len_ref, q_ref, qn_ref, h_ref, ahead_ref, back_ref, dzq_ref, segc_ref, segr_ref):
    rows = q_ref.shape[0]
    layout = Layout(len_ref, rows, tokens)

    @pl.when(pl.program_id(0) == 0)
    def _():
        segment_columns(segc_ref, layout, 0, rows)
        segment_rows(segr_ref, layout)

    q_ext = jnp.concatenate([q_ref[...], qn_ref[...]], axis=0)
    dzq_ref[...] = jnp.zeros_like(dzq_ref)
    first, end = layout.span()

    def one_segment(s, carry):
        spectrum = dot(kept(ahead_ref[...], segc_ref[...], s), q_ext)
        g = conj_times(h_ref[...], spectrum, rows).astype(BF)
        dzq_ref[...] += dot(kept(back_ref[...], segr_ref[...], s), g)
        return carry

    lax.fori_loop(first, end, one_segment, 0)


def w_kernel(tokens, len_ref, z_ref, zp_ref, h_ref, behind_ref, back_ref, w_ref, segc_ref, segr_ref):
    rows = z_ref.shape[0]
    layout = Layout(len_ref, rows, tokens)

    @pl.when(pl.program_id(0) == 0)
    def _():
        segment_columns(segc_ref, layout, 0, -rows)
        segment_rows(segr_ref, layout)

    z_ext = jnp.concatenate([z_ref[...], zp_ref[...]], axis=0)
    w_ref[...] = jnp.zeros_like(w_ref)
    first, end = layout.span()

    def one_segment(s, carry):
        spectrum = dot(kept(behind_ref[...], segc_ref[...], s), z_ext)
        g = times(h_ref[...], spectrum, rows).astype(BF)
        w_ref[...] += dot(kept(back_ref[...], segr_ref[...], s), g)
        return carry

    lax.fori_loop(first, end, one_segment, 0)


def dzu_kernel(tokens, len_ref, q_ref, qn_ref, up_ref, upn_ref, h_ref, z_ref, a_ref, ahead_ref, own_ref, back_ref,
               dzu_ref, total_ref, segc_ref, segr_ref):
    rows = q_ref.shape[0]
    layout = Layout(len_ref, rows, tokens)

    @pl.when(pl.program_id(0) == 0)
    def _():
        segment_columns(segc_ref, layout, 0, rows)
        segment_rows(segr_ref, layout)

    own = (q_ref[...].astype(F32) * up_ref[...].astype(F32)).astype(BF)
    rim = (qn_ref[...].astype(F32) * upn_ref[...].astype(F32)).astype(BF)
    u_ext = jnp.concatenate([own, rim], axis=0)
    dzu_ref[...] = jnp.zeros_like(dzu_ref)
    first, end = layout.span()
    z_spec = dot(kept(own_ref[...], segc_ref[:, :rows], end - 1), z_ref[...])
    rim_spec = dot(kept(ahead_ref[:, rows:], segc_ref[:, rows:], end - 1), rim)
    total_ref[...] = a_ref[...] + conj_times(z_spec, rim_spec, rows)

    def one_segment(s, carry):
        spectrum = dot(kept(ahead_ref[...], segc_ref[...], s), u_ext)
        g = conj_times(h_ref[...], spectrum, rows).astype(BF)
        dzu_ref[...] += dot(kept(back_ref[...], segr_ref[...], s), g)
        return carry

    lax.fori_loop(first, end, one_segment, 0)


def coefficients(len_ref, ids_ref, part_ref):
    count = len_ref.shape[0]
    index = lax.broadcasted_iota(jnp.int32, (count, 128), 0)
    length = jnp.zeros((count, 128), F32)
    ids = jnp.zeros((count, 128), jnp.int32)
    for s in range(count):
        length = jnp.where(index == s, len_ref[s].astype(F32), length)
        ids = jnp.where(index == s, ids_ref[s], ids)
    scores = jnp.broadcast_to(jnp.sum(part_ref[...], axis=1, keepdims=True), (count, 128)) / length
    total = jnp.zeros((count, 128), F32)
    mates = jnp.zeros((count, 128), F32)
    for s in range(count):
        same = jnp.where(ids == ids_ref[s], 1.0, 0.0)
        mates = mates + same
        total = total + same * scores[s : s + 1, :]
    return (scores - total / mates) / length


def token_coefficients(coef, seg):
    spread = jnp.zeros(seg.shape, F32)
    for s in range(coef.shape[0]):
        spread = jnp.where(seg == s, coef[s : s + 1, :], spread)
    return spread


def across(column, width):
    return jnp.concatenate([column] * (width // 128), axis=1)


def grads_kernel(tokens, sub_ref, len_ref, ids_ref, part_ref, s_ref, halo_ref, q_ref, k_ref, v_ref, up_ref, dir_ref,
                 w_ref, dzu_ref, dzq_ref, a_ref, rim_ref, cross_ref, back_ref,
                 da_ref, head_ref, send_ref, keep_ref, sm_ref, coef_ref, tok_ref, acc_ref, slot_ref, sems):
    rows, width = q_ref.shape
    layout = Layout(len_ref, rows, tokens)
    step = pl.program_id(0)
    steps = pl.num_programs(0)
    half = steps // 2
    at = lax.rem(step + (1 - sub_ref[0]) * half, steps)
    first, end = layout.span()

    def fetch(s, carry):
        cross_copy(cross_ref, slot_ref, sems, s, at, width).start()
        return carry

    lax.fori_loop(first, end, fetch, 0)

    @pl.when(step == 0)
    def _():
        causal_shifts(sm_ref, layout, 0)
        coef = coefficients(len_ref, ids_ref, part_ref)
        coef_ref[...] = coef
        position = layout.base + lax.broadcasted_iota(jnp.int32, (rows, 128), 0)
        tok_ref[...] = token_coefficients(coef, layout.segment(position))

    rise = across(tok_ref[...], width) * dir_ref[...]
    dz = dzu_ref[...] + rise * dzq_ref[...]
    dq = ((up_ref[...].astype(F32) + rise) * w_ref[...]).astype(BF)
    dk = (dz * v_ref[...].astype(F32)).astype(BF)
    dv = (dz * k_ref[...].astype(F32)).astype(BF)
    blocks = []
    for i, da in enumerate((dq, dk, dv)):
        da_ref[i] = da
        head_ref[i] = da[:RIM]
        grad = da.astype(F32)
        x = jnp.concatenate([halo_ref[i], s_ref[i]], axis=0)
        moved = dot(sm_ref[...], x)
        sums = [jnp.sum(grad * s_ref[i].astype(F32), axis=0, keepdims=True)]
        for j in range(1, KF):
            sums.append(jnp.sum(grad * moved[(j - 1) * rows : j * rows], axis=0, keepdims=True))
        sums.append(jnp.zeros_like(sums[0]))
        blocks.append(jnp.concatenate(sums, axis=0))

    def weight(s):
        return across(coef_ref[pl.ds(s, 1), :], width) * dir_ref[...]

    acc_ref[...] = a_ref[...] + weight(end - 1) * rim_ref[...].astype(F32)

    def one_segment(s, carry):
        cross_copy(cross_ref, slot_ref, sems, s, at, width).wait()
        acc_ref[...] += weight(s) * slot_ref[s].astype(F32)
        return carry

    lax.fori_loop(first, end, one_segment, 0)
    result = jnp.concatenate([dot(back_ref[...].astype(BF), acc_ref[...].astype(BF))] + blocks, axis=0)

    @pl.when(step < half)
    def _():
        send_ref[...] = result.astype(BF)

    @pl.when(step >= half)
    def _():
        keep_ref[...] = result


def dstreams_kernel(tokens, len_ref, da_ref, rim_ref, taps_ref, out_ref, sm_ref):
    rows = da_ref.shape[1]

    @pl.when(pl.program_id(0) == 0)
    def _():
        reverse_shifts(sm_ref, Layout(len_ref, rows, tokens))

    for i in range(3):
        x = jnp.concatenate([da_ref[i], rim_ref[i]], axis=0)
        out_ref[i] = tap_sum(sm_ref, taps_ref[i], da_ref[i], x, rows).astype(BF)


def shares_kernel(keep_ref, recv_ref, own_ref, *share_refs):
    count = len(share_refs) + 1
    shard = own_ref.shape[0] - FEAT_ROWS
    taps = keep_ref.shape[0] - FEAT_ROWS
    feat = (keep_ref[taps:, :] + recv_ref[taps:, :].astype(F32)).astype(BF)
    for d in range(count):
        at = pl.ds(pl.multiple_of(lax.rem(lax.axis_index("ctx") + d, count) * shard, 8), shard)
        total = keep_ref[at, :] + recv_ref[at, :].astype(F32)
        ref = own_ref if d == 0 else share_refs[d - 1]
        ref[:shard, :] = total.astype(ref.dtype)
        ref[shard:, :] = feat.astype(ref.dtype)


def finish_kernel(own_ref, *refs):
    shares, (out_ref, slot_ref) = refs[:-2], refs[-2:]
    count = len(shares) + 1
    shard = own_ref.shape[0] - FEAT_ROWS
    total = own_ref[:shard, :]
    for share in shares:
        total = total + share[:shard, :].astype(F32)
    out_ref[:shard, :] = total
    for d, share in enumerate((own_ref, *shares)):
        slot_ref[lax.rem(lax.axis_index("ctx") + (count - d), count)] = share[shard:, :].astype(F32)
    total = slot_ref[0]
    for d in range(1, count):
        total = total + slot_ref[d]
    out_ref[shard:, :] = total


def joined_kernel(mine_ref, other_ref, dfilt_ref, dfeat_ref):
    shard, width = dfilt_ref.shape[0], mine_ref.shape[1]
    here = pl.multiple_of(lax.axis_index("sub") * width, 128)
    there = pl.multiple_of((1 - lax.axis_index("sub")) * width, 128)
    for at, half in ((here, mine_ref), (there, other_ref)):
        dfilt_ref[:, pl.ds(at, width)] = half[:shard, :]
        for i in range(3):
            dfeat_ref[i, :, pl.ds(at, width)] = half[shard + 8 * i : shard + 8 * i + KF, :]


def local(streams, feat_taps, long_filter, upstream, score_dir, seg_lengths, list_ids):
    rows, chans = streams.shape[1:]
    segs = seg_lengths.shape[0]
    shard = long_filter.shape[0]
    ring = ("ctx", "sub")
    tokens = rows * lax.axis_size("ctx") * lax.axis_size("sub")
    shards = lax.axis_size("ctx")
    tile = min(512, chans // 2)
    steps = chans // tile
    half = steps // 2
    ahead, behind, own_wave, back = half_wave(rows)
    after = ahead[:, rows:]
    ahead, behind, own_wave, back, after = (jnp.asarray(t) for t in (ahead, behind, own_wave, back, after))
    sub_of = lax.axis_index("sub").astype(jnp.int32).reshape(1)
    direction = score_dir.reshape(1, chans)

    smem = pl.BlockSpec(memory_space=pltpu.SMEM)
    anywhere = pl.BlockSpec(memory_space=pl.ANY)
    blk = lambda *shape: pl.BlockSpec((*shape, tile), lambda i: (0,) * len(shape) + (i,))
    whole = lambda *shape: pl.BlockSpec(shape, lambda i: (0,) * len(shape))
    out = lambda dtype, *shape: jax.ShapeDtypeStruct(shape, dtype)
    vmem = lambda dtype, *shape: pltpu.VMEM(shape, dtype)
    params = pltpu.CompilerParams(vmem_limit_bytes=VMEM_LIMIT)
    cost = lambda us: pl.CostEstimate(flops=int(us * 1e9), bytes_accessed=int(us * 3e6), transcendentals=0)
    shifts = vmem(BF, (KF - 1) * rows, rows + RIM)
    wide, tall = vmem(F32, 2 * rows, 2 * rows), vmem(F32, rows, 2 * rows)

    sq, tails, part = pl.pallas_call(
        cut_kernel,
        in_specs=[anywhere, anywhere], out_specs=[anywhere] * 3,
        out_shape=[out(BF, rows, chans), out(BF, 3, RIM, chans), out(BF, shard, chans // 2)],
        scratch_shapes=[pltpu.SemaphoreType.DMA((3,))],
        compiler_params=params, cost_estimate=cost(1), name="cut",
    )(streams, long_filter)
    halo = passed_along(tails, ring, 1)
    mine = jnp.stack([part] + [rotated(part, "ctx", d) for d in range(1, shards)])
    sq_next = passed_along(sq, ring, -1)

    query, key_feat, value_feat, product = pl.pallas_call(
        lambda *refs: feat_kernel(tokens, *refs),
        grid=(steps,),
        in_specs=[smem, blk(3, rows), blk(3, RIM), blk(3, KF)],
        out_specs=[blk(rows)] * 4,
        out_shape=[out(BF, rows, chans)] * 4,
        scratch_shapes=[shifts],
        compiler_params=params, cost_estimate=cost(3), name="feats",
    )(seg_lengths, streams, halo, feat_taps)
    z_prev = passed_along(product, ring, 1)

    cross, a_own = pl.pallas_call(
        lambda *refs: spectra_kernel(tokens, *refs),
        grid=(steps,),
        in_specs=[smem, blk(rows), blk(rows), blk(rows), whole(2 * rows, rows)],
        out_specs=[anywhere, blk(2 * rows)],
        out_shape=[out(BF, segs, 2 * rows, chans), out(F32, 2 * rows, chans)],
        scratch_shapes=[vmem(F32, 2 * rows, rows), vmem(BF, segs, 2 * rows, tile), pltpu.SemaphoreType.DMA((segs,))],
        compiler_params=params, cost_estimate=cost(6), name="own_spectra",
    )(seg_lengths, product, query, upstream, own_wave)

    other = swapped(mine, "sub", 1)
    up_held, _ = lax.optimization_barrier((upstream, mine))
    up_next = passed_along(up_held, ring, -1)

    half_blk = pl.BlockSpec((shards, shard, tile), lambda i: (0, 0, i % half))
    q_next, spectrum, rim_cross, partial = pl.pallas_call(
        lambda *refs: score_kernel(tokens, *refs),
        grid=(steps,),
        in_specs=[smem, pl.BlockSpec((1, RIM, tile), lambda i: (0, rows // RIM - 1, i)), blk(rows), blk(3, KF),
                  half_blk, half_blk, blk(rows), blk(1), anywhere, whole(2 * rows, rows), whole(2 * rows, rows)],
        out_specs=[blk(rows), blk(2 * rows), blk(2 * rows), whole(segs, 128)],
        out_shape=[out(BF, rows, chans), out(F32, 2 * rows, chans), out(BF, 2 * rows, chans), out(F32, segs, 128)],
        scratch_shapes=[shifts, wide, vmem(F32, LH, tile), vmem(BF, segs, 2 * rows, tile), pltpu.SemaphoreType.DMA((segs,))],
        compiler_params=params, cost_estimate=cost(3), name="scores",
    )(seg_lengths, streams, sq_next, feat_taps, mine, other, product, direction, cross, after, own_wave)

    totals = summed_everywhere(partial)

    dzq = pl.pallas_call(
        lambda *refs: dzq_kernel(tokens, *refs),
        grid=(steps,),
        in_specs=[smem, blk(rows), blk(rows), blk(2 * rows), whole(2 * rows, 2 * rows), whole(rows, 2 * rows)],
        out_specs=blk(rows),
        out_shape=out(F32, rows, chans),
        scratch_shapes=[wide, tall],
        compiler_params=params, cost_estimate=cost(3), name="adjoint_of_q",
    )(seg_lengths, query, q_next, spectrum, ahead, back)

    mixed = pl.pallas_call(
        lambda *refs: w_kernel(tokens, *refs),
        grid=(steps,),
        in_specs=[smem, blk(rows), blk(rows), blk(2 * rows), whole(2 * rows, 2 * rows), whole(rows, 2 * rows)],
        out_specs=blk(rows),
        out_shape=out(F32, rows, chans),
        scratch_shapes=[wide, tall],
        compiler_params=params, cost_estimate=cost(3), name="mixed",
    )(seg_lengths, product, z_prev, spectrum, behind, back)

    dzu, a_total = pl.pallas_call(
        lambda *refs: dzu_kernel(tokens, *refs),
        grid=(steps,),
        in_specs=[smem, blk(rows), blk(rows), blk(rows), blk(rows), blk(2 * rows), blk(rows), blk(2 * rows),
                  whole(2 * rows, 2 * rows), whole(2 * rows, rows), whole(rows, 2 * rows)],
        out_specs=[blk(rows), blk(2 * rows)],
        out_shape=[out(F32, rows, chans), out(F32, 2 * rows, chans)],
        scratch_shapes=[wide, tall],
        compiler_params=params, cost_estimate=cost(4), name="adjoint_of_up",
    )(seg_lengths, query, q_next, upstream, up_next, spectrum, product, a_own, ahead, own_wave, back)

    turned = lambda i, ref: lax.rem(i + (1 - ref[0]) * half, steps)
    tblk = lambda *shape: pl.BlockSpec((*shape, tile), lambda i, ref: (0,) * len(shape) + (turned(i, ref),))
    twhole = lambda *shape: pl.BlockSpec(shape, lambda i, ref: (0,) * len(shape))
    tsend = lambda *shape: pl.BlockSpec((*shape, tile), lambda i, ref: (0,) * len(shape) + (jnp.minimum(i, half - 1),))
    tkeep = lambda *shape: pl.BlockSpec((*shape, tile), lambda i, ref: (0,) * len(shape) + (jnp.maximum(i - half, 0),))

    grads, heads, send, keep = pl.pallas_call(
        lambda *refs: grads_kernel(tokens, *refs),
        grid_spec=pltpu.PrefetchScalarGridSpec(
            num_scalar_prefetch=1, grid=(steps,),
            in_specs=[smem, smem, twhole(segs, 128), tblk(3, rows), tblk(3, RIM)] + [tblk(rows)] * 4 + [tblk(1)]
            + [tblk(rows)] * 3 + [tblk(2 * rows)] * 2 + [anywhere, twhole(rows, 2 * rows)],
            out_specs=[tblk(3, rows), tblk(3, RIM), tsend(LH + FEAT_ROWS), tkeep(LH + FEAT_ROWS)],
            scratch_shapes=[shifts, vmem(F32, segs, 128), vmem(F32, rows, 128), vmem(F32, 2 * rows, tile),
                            vmem(BF, segs, 2 * rows, tile), pltpu.SemaphoreType.DMA((segs,))],
        ),
        out_shape=[out(BF, 3, rows, chans), out(BF, 3, RIM, chans), out(BF, LH + FEAT_ROWS, chans // 2),
                   out(F32, LH + FEAT_ROWS, chans // 2)],
        compiler_params=params, cost_estimate=cost(5), name="gradients",
    )(sub_of, seg_lengths, list_ids, totals, streams, halo, query, key_feat, value_feat, upstream, direction,
      mixed, dzu, dzq, a_total, rim_cross, cross, back)
    received = swapped(send, "sub", 1)
    shares = pl.pallas_call(
        shares_kernel,
        out_shape=[out(F32, shard + FEAT_ROWS, chans // 2)] + [out(BF, shard + FEAT_ROWS, chans // 2)] * (shards - 1),
        compiler_params=params, cost_estimate=cost(1), name="shares",
    )(keep, received)
    parts = [rotated(shares[d], "ctx", d) for d in range(1, shards)]
    rim = passed_along(heads, ring, -1)

    d_streams = pl.pallas_call(
        lambda *refs: dstreams_kernel(tokens, *refs),
        grid=(steps,),
        in_specs=[smem, blk(3, rows), blk(3, RIM), blk(3, KF)],
        out_specs=blk(3, rows),
        out_shape=out(BF, 3, rows, chans),
        scratch_shapes=[shifts],
        compiler_params=params, cost_estimate=cost(4), name="stream_grads",
    )(seg_lengths, grads, rim, feat_taps)

    summed = pl.pallas_call(
        finish_kernel,
        out_shape=out(F32, shard + FEAT_ROWS, chans // 2),
        scratch_shapes=[vmem(F32, shards, FEAT_ROWS, chans // 2)],
        compiler_params=params, cost_estimate=cost(1), name="shard_sums",
    )(*shares[:1], *parts)
    d_filter, d_feat = pl.pallas_call(
        joined_kernel,
        out_shape=[out(F32, shard, chans), out(F32, 3, KF, chans)],
        compiler_params=params, cost_estimate=cost(1), name="both_halves",
    )(summed, swapped(summed, "sub", 1))
    return (d_streams, d_feat, d_filter)


def solution(mesh):
    placed = (
        P(None, ("groups", "ctx", "sub"), "fsdp"),
        P(None, None, "fsdp"),
        P("ctx", "fsdp"),
        P(("groups", "ctx", "sub"), "fsdp"),
        P("fsdp"),
        P("groups"),
        P("groups"),
    )
    return jax.shard_map(
        local,
        mesh=mesh,
        in_specs=placed,
        out_specs=(
            P(None, ("groups", "ctx", "sub"), "fsdp"),
            P("groups", None, "fsdp"),
            P(("groups", "ctx"), "fsdp"),
        ),
        check_vma=False,
    )
```

```python
import jax
import jax.numpy as jnp
import numpy as np
from jax import lax
from jax.experimental import pallas as pl
from jax.experimental.pallas import tpu as pltpu
from jax.sharding import PartitionSpec as P

LH = 128
KF = 7
RIM = 16
FEAT_ROWS = 24
BF = jnp.bfloat16
F32 = jnp.float32
VMEM_LIMIT = 24 * 1024 * 1024
TILE = 512


def passed_along(value, axis, steps):
    count = lax.axis_size(axis)
    leading, last = (max(0, -steps), min(count, count - steps))
    return lax.ppermute(value, axis, [(source, source + steps) for source in range(leading, last)])


def swapped(value, axis, distance):
    count = lax.axis_size(axis)
    return lax.ppermute(value, axis, [(source, source ^ distance) for source in range(count)])


def rotated(value, axis, distance):
    count = lax.axis_size(axis)
    return lax.ppermute(value, axis, [(source, (source + distance) % count) for source in range(count)])


def half_wave(rows):
    odd = 2 * np.arange(rows)[:, None] + 1
    span = np.arange(-rows, 2 * rows)[None, :]
    angle = np.pi * ((odd * span) % (4 * rows)) / (2 * rows)
    table = np.concatenate([np.cos(angle), -np.sin(angle)], axis=0)
    before, own, after = np.split(table, 3, axis=1)
    back = own.T / rows
    as_f32 = lambda parts: np.concatenate(parts, axis=1).astype(np.float32)
    return as_f32([own, after]), as_f32([own, before]), as_f32([own]), as_f32([back])


def dot(left, right):
    return jnp.dot(left, right, preferred_element_type=F32)


class Layout:
    def __init__(self, len_ref, rows, tokens):
        self.rows, self.tokens = rows, tokens
        self.count = len_ref.shape[0]
        self.base = (lax.axis_index("ctx") * lax.axis_size("sub") + lax.axis_index("sub")) * rows
        offset = jnp.int32(0)
        self.offsets = []
        for s in range(self.count):
            self.offsets.append(offset)
            offset = offset + len_ref[s]

    def segment(self, position):
        seg = jnp.zeros_like(position)
        for s in range(1, self.count):
            seg = seg + jnp.where(position >= self.offsets[s], 1, 0)
        return jnp.where((position >= 0) & (position < self.tokens), seg, -1)

    def age(self, position):
        start = jnp.zeros_like(position)
        for s in range(1, self.count):
            start = jnp.where(position >= self.offsets[s], self.offsets[s], start)
        return position - start

    def scalar_segment(self, position):
        seg = jnp.int32(0)
        for s in range(1, self.count):
            seg = seg + jnp.where(position >= self.offsets[s], 1, 0)
        return seg

    def span(self):
        return self.scalar_segment(self.base), self.scalar_segment(self.base + self.rows - 1) + 1


def tiles(chans):
    tile = min(TILE, chans)
    return [pl.ds(c, tile) for c in range(0, chans, tile)]


def causal_shifts(sm_ref, layout, first):
    rows = layout.rows
    row = lax.broadcasted_iota(jnp.int32, (rows, rows + RIM), 0)
    col = lax.broadcasted_iota(jnp.int32, (rows, rows + RIM), 1)
    age = layout.age(layout.base + first + row)
    for j in range(1, KF):
        hit = (col == row + (RIM - j)) & (age >= j)
        sm_ref[(j - 1) * rows : j * rows, :] = jnp.where(hit, 1.0, 0.0).astype(BF)


def reverse_shifts(sm_ref, layout):
    rows = layout.rows
    row = lax.broadcasted_iota(jnp.int32, (rows, rows + RIM), 0)
    col = lax.broadcasted_iota(jnp.int32, (rows, rows + RIM), 1)
    age = layout.age(layout.base + col)
    for j in range(1, KF):
        hit = (col == row + j) & (age >= j)
        sm_ref[(j - 1) * rows : j * rows, :] = jnp.where(hit, 1.0, 0.0).astype(BF)


def tap_sum(sm_ref, taps, here, x, rows):
    total = here.astype(F32) * taps[0:1, :]
    moved = dot(sm_ref[...], x)
    for j in range(1, KF):
        total = total + moved[(j - 1) * rows : j * rows] * taps[j : j + 1, :]
    return total


def cut_kernel(streams_ref, filter_ref, query_ref, tail_ref, half_ref, sems):
    rows = streams_ref.shape[1]
    width = half_ref.shape[1]
    at = pl.multiple_of(lax.axis_index("sub") * width, 128)
    copies = [
        pltpu.make_async_copy(streams_ref.at[:, pl.ds(rows - RIM, RIM), :], tail_ref, sems.at[0]),
        pltpu.make_async_copy(filter_ref.at[:, pl.ds(at, width)], half_ref, sems.at[1]),
        pltpu.make_async_copy(streams_ref.at[0], query_ref, sems.at[2]),
    ]
    for copy in copies:
        copy.start()
    for copy in copies:
        copy.wait()


def feat_kernel(tokens, len_ref, s_ref, halo_ref, taps_ref, q_ref, k_ref, v_ref, z_ref, sm_ref):
    rows = s_ref.shape[1]
    causal_shifts(sm_ref, Layout(len_ref, rows, tokens), 0)
    for c in tiles(s_ref.shape[2]):
        feats = []
        for i, out in enumerate((q_ref, k_ref, v_ref)):
            here = s_ref[i, :, c]
            x = jnp.concatenate([halo_ref[i, :, c], here], axis=0)
            feat = tap_sum(sm_ref, taps_ref[i, :, c], here, x, rows).astype(BF)
            out[:, c] = feat
            feats.append(feat)
        z_ref[:, c] = (feats[1].astype(F32) * feats[2].astype(F32)).astype(BF)


def segment_columns(layout, shape, first_own, first_rim):
    rows = layout.rows
    col = lax.broadcasted_iota(jnp.int32, shape, 1)
    return layout.segment(layout.base + jnp.where(col < rows, col + first_own, col - rows + first_rim))


def segment_rows(layout, shape):
    return layout.segment(layout.base + lax.broadcasted_iota(jnp.int32, shape, 0))


def kept(table, seg_table, s):
    return jnp.where(seg_table == s, table, 0.0).astype(BF)


def times(a, b, rows):
    ar, ai, br, bi = a[:rows], a[rows:], b[:rows], b[rows:]
    return jnp.concatenate([ar * br - ai * bi, ar * bi + ai * br], axis=0)


def conj_times(a, b, rows):
    ar, ai, br, bi = a[:rows], a[rows:], b[:rows], b[rows:]
    return jnp.concatenate([ar * br + ai * bi, ar * bi - ai * br], axis=0)


def spectra_kernel(tokens, len_ref, z_ref, q_ref, up_ref, own_ref, cross_ref, a_ref, segc_ref):
    rows, chans = z_ref.shape
    layout = Layout(len_ref, rows, tokens)
    segc_ref[...] = segment_columns(layout, segc_ref.shape, 0, rows)
    a_ref[...] = jnp.zeros_like(a_ref)
    first, end = layout.span()

    def one_segment(s, carry):
        wave = kept(own_ref[...], segc_ref[...], s)
        for c in tiles(chans):
            z_spec = dot(wave, z_ref[:, c])
            q = q_ref[:, c]
            u = (q.astype(F32) * up_ref[:, c].astype(F32)).astype(BF)
            cross_ref[s, :, c] = conj_times(z_spec, dot(wave, q), rows).astype(BF)
            a_ref[:, c] += conj_times(z_spec, dot(wave, u), rows)
        return carry

    lax.fori_loop(first, end, one_segment, 0)


def score_kernel(tokens, len_ref, s_ref, sqn_ref, taps_ref, mine_ref, other_ref, z_ref, dir_ref, cross_ref,
                 after_ref, own_ref, qn_ref, h_ref, rim_ref, part_ref, sm_ref, filt_ref):
    rows, chans = z_ref.shape
    layout = Layout(len_ref, rows, tokens)
    first, end = layout.span()
    causal_shifts(sm_ref, layout, rows)
    own, wave = own_ref[...].astype(BF), kept(own_ref[...], segment_columns(layout, own_ref.shape, 0, rows), end - 1)
    after = kept(after_ref[...], segment_columns(layout, after_ref.shape, rows, rows), end - 1)
    part_ref[...] = jnp.zeros_like(part_ref)

    def add(s, c, cross):
        row = jnp.sum(h_ref[:, c] * cross, axis=0, keepdims=True) * dir_ref[:, c] * (1.0 / rows)
        lanes = row[:, :128]
        for n in range(128, row.shape[1], 128):
            lanes = lanes + row[:, n : n + 128]
        part_ref[pl.ds(s, 1), :] += lanes

    shards, shard, width = mine_ref.shape
    for ref, half in ((mine_ref, lax.axis_index("sub")), (other_ref, 1 - lax.axis_index("sub"))):
        at = pl.ds(pl.multiple_of(half * width, 128), width)
        for d in range(shards):
            row = lax.rem(lax.axis_index("ctx") + (shards - d), shards) * shard
            filt_ref[pl.ds(pl.multiple_of(row, 8), shard), at] = ref[d].astype(F32)
    for c in tiles(chans):
        here = sqn_ref[:, c]
        x = jnp.concatenate([s_ref[0, rows - RIM :, c], here], axis=0)
        qn = tap_sum(sm_ref, taps_ref[0, :, c], here, x, rows).astype(BF)
        qn_ref[:, c] = qn
        h_ref[:, c] = dot(own, filt_ref[:, c].astype(BF))
        rim = conj_times(dot(wave, z_ref[:, c]), dot(after, qn), rows)
        rim_ref[:, c] = rim.astype(BF)
        add(end - 1, c, rim)

    def one_segment(s, carry):
        for c in tiles(chans):
            add(s, c, cross_ref[s, :, c].astype(F32))
        return carry

    lax.fori_loop(first, end, one_segment, 0)


def dzq_kernel(tokens, len_ref, q_ref, qn_ref, h_ref, ahead_ref, back_ref, dzq_ref, segc_ref, segr_ref):
    rows, chans = q_ref.shape
    layout = Layout(len_ref, rows, tokens)
    segc_ref[...] = segment_columns(layout, segc_ref.shape, 0, rows)
    segr_ref[...] = segment_rows(layout, segr_ref.shape)
    dzq_ref[...] = jnp.zeros_like(dzq_ref)

    def one_segment(s, carry):
        wave, back = kept(ahead_ref[...], segc_ref[...], s), kept(back_ref[...], segr_ref[...], s)
        for c in tiles(chans):
            spectrum = dot(wave, jnp.concatenate([q_ref[:, c], qn_ref[:, c]], axis=0))
            dzq_ref[:, c] += dot(back, conj_times(h_ref[:, c], spectrum, rows).astype(BF))
        return carry

    lax.fori_loop(*layout.span(), one_segment, 0)


def w_kernel(tokens, len_ref, z_ref, zp_ref, h_ref, behind_ref, back_ref, w_ref, segc_ref, segr_ref):
    rows, chans = z_ref.shape
    layout = Layout(len_ref, rows, tokens)
    segc_ref[...] = segment_columns(layout, segc_ref.shape, 0, -rows)
    segr_ref[...] = segment_rows(layout, segr_ref.shape)
    w_ref[...] = jnp.zeros_like(w_ref)

    def one_segment(s, carry):
        wave, back = kept(behind_ref[...], segc_ref[...], s), kept(back_ref[...], segr_ref[...], s)
        for c in tiles(chans):
            spectrum = dot(wave, jnp.concatenate([z_ref[:, c], zp_ref[:, c]], axis=0))
            w_ref[:, c] += dot(back, times(h_ref[:, c], spectrum, rows).astype(BF))
        return carry

    lax.fori_loop(*layout.span(), one_segment, 0)


def dzu_kernel(tokens, len_ref, q_ref, qn_ref, up_ref, upn_ref, h_ref, z_ref, a_ref, ahead_ref, own_ref, back_ref,
               dzu_ref, total_ref, segc_ref, segr_ref, u_ref):
    rows, chans = q_ref.shape
    layout = Layout(len_ref, rows, tokens)
    segc_ref[...] = segment_columns(layout, segc_ref.shape, 0, rows)
    segr_ref[...] = segment_rows(layout, segr_ref.shape)
    first, end = layout.span()
    wave = kept(own_ref[...], segc_ref[:, :rows], end - 1)
    after = kept(ahead_ref[:, rows:], segc_ref[:, rows:], end - 1)
    for c in tiles(chans):
        u_ref[:rows, c] = (q_ref[:, c].astype(F32) * up_ref[:, c].astype(F32)).astype(BF)
        rim = (qn_ref[:, c].astype(F32) * upn_ref[:, c].astype(F32)).astype(BF)
        u_ref[rows:, c] = rim
        total_ref[:, c] = a_ref[:, c] + conj_times(dot(wave, z_ref[:, c]), dot(after, rim), rows)
    dzu_ref[...] = jnp.zeros_like(dzu_ref)

    def one_segment(s, carry):
        wave, back = kept(ahead_ref[...], segc_ref[...], s), kept(back_ref[...], segr_ref[...], s)
        for c in tiles(chans):
            spectrum = dot(wave, u_ref[:, c])
            dzu_ref[:, c] += dot(back, conj_times(h_ref[:, c], spectrum, rows).astype(BF))
        return carry

    lax.fori_loop(first, end, one_segment, 0)


def coefficients(len_ref, ids_ref, part_ref):
    count = len_ref.shape[0]
    index = lax.broadcasted_iota(jnp.int32, (count, 128), 0)
    length = jnp.zeros((count, 128), F32)
    ids = jnp.zeros((count, 128), jnp.int32)
    for s in range(count):
        length = jnp.where(index == s, len_ref[s].astype(F32), length)
        ids = jnp.where(index == s, ids_ref[s], ids)
    scores = jnp.broadcast_to(jnp.sum(part_ref[...], axis=1, keepdims=True), (count, 128)) / length
    total = jnp.zeros((count, 128), F32)
    mates = jnp.zeros((count, 128), F32)
    for s in range(count):
        same = jnp.where(ids == ids_ref[s], 1.0, 0.0)
        mates = mates + same
        total = total + same * scores[s : s + 1, :]
    return (scores - total / mates) / length


def token_coefficients(coef, seg):
    spread = jnp.zeros(seg.shape, F32)
    for s in range(coef.shape[0]):
        spread = jnp.where(seg == s, coef[s : s + 1, :], spread)
    return spread


def across(column, width):
    return jnp.concatenate([column] * (width // 128), axis=1)


def grads_kernel(tokens, len_ref, ids_ref, part_ref, s_ref, halo_ref, q_ref, k_ref, v_ref, up_ref, dir_ref,
                 w_ref, dzu_ref, dzq_ref, a_ref, rim_ref, cross_ref, back_ref,
                 da_ref, head_ref, send_ref, keep_ref, sm_ref, coef_ref, tok_ref, acc_ref):
    rows, chans = q_ref.shape
    layout = Layout(len_ref, rows, tokens)
    first, end = layout.span()
    causal_shifts(sm_ref, layout, 0)
    coef = coefficients(len_ref, ids_ref, part_ref)
    coef_ref[...] = coef
    tok_ref[...] = token_coefficients(coef, segment_rows(layout, (rows, 128)))
    last = across(coef_ref[pl.ds(end - 1, 1), :], chans) * dir_ref[...]
    for c in tiles(chans):
        acc_ref[:, c] = a_ref[:, c] + last[:, c.start : c.start + c.size] * rim_ref[:, c].astype(F32)

    def one_segment(s, carry):
        weight = across(coef_ref[pl.ds(s, 1), :], chans) * dir_ref[...]
        for c in tiles(chans):
            acc_ref[:, c] += weight[:, c.start : c.start + c.size] * cross_ref[s, :, c].astype(F32)
        return carry

    lax.fori_loop(first, end, one_segment, 0)

    width = chans // 2
    tile = min(TILE, width)
    for ref, half in ((send_ref, 1 - lax.axis_index("sub")), (keep_ref, lax.axis_index("sub"))):
        for start in range(0, width, tile):
            c = pl.ds(pl.multiple_of(half * width + start, 128), tile)
            direction = dir_ref[:, c]
            rise = across(tok_ref[...], tile) * direction
            dz = dzu_ref[:, c] + rise * dzq_ref[:, c]
            dq = ((up_ref[:, c].astype(F32) + rise) * w_ref[:, c]).astype(BF)
            dk = (dz * v_ref[:, c].astype(F32)).astype(BF)
            dv = (dz * k_ref[:, c].astype(F32)).astype(BF)
            blocks = [dot(back_ref[...].astype(BF), acc_ref[:, c].astype(BF))]
            for i, da in enumerate((dq, dk, dv)):
                da_ref[i, :, c] = da
                head_ref[i, :, c] = da[:RIM]
                grad = da.astype(F32)
                here = s_ref[i, :, c]
                moved = dot(sm_ref[...], jnp.concatenate([halo_ref[i, :, c], here], axis=0))
                sums = [jnp.sum(grad * here.astype(F32), axis=0, keepdims=True)]
                for j in range(1, KF):
                    sums.append(jnp.sum(grad * moved[(j - 1) * rows : j * rows], axis=0, keepdims=True))
                sums.append(jnp.zeros_like(sums[0]))
                blocks.append(jnp.concatenate(sums, axis=0))
            ref[:, start : start + tile] = jnp.concatenate(blocks, axis=0).astype(ref.dtype)


def dstreams_kernel(tokens, len_ref, da_ref, rim_ref, taps_ref, out_ref, sm_ref):
    rows, chans = da_ref.shape[1:]
    reverse_shifts(sm_ref, Layout(len_ref, rows, tokens))
    for c in tiles(chans):
        for i in range(3):
            here = da_ref[i, :, c]
            x = jnp.concatenate([here, rim_ref[i, :, c]], axis=0)
            out_ref[i, :, c] = tap_sum(sm_ref, taps_ref[i, :, c], here, x, rows).astype(BF)


def shares_kernel(keep_ref, recv_ref, own_ref, *share_refs):
    count = len(share_refs) + 1
    shard = own_ref.shape[0] - FEAT_ROWS
    taps = keep_ref.shape[0] - FEAT_ROWS
    feat = (keep_ref[taps:, :] + recv_ref[taps:, :].astype(F32)).astype(BF)
    for d in range(count):
        at = pl.ds(pl.multiple_of(lax.rem(lax.axis_index("ctx") + d, count) * shard, 8), shard)
        total = keep_ref[at, :] + recv_ref[at, :].astype(F32)
        ref = own_ref if d == 0 else share_refs[d - 1]
        ref[:shard, :] = total.astype(ref.dtype)
        ref[shard:, :] = feat.astype(ref.dtype)


def finish_kernel(own_ref, *refs):
    shares, (out_ref, slot_ref) = refs[:-2], refs[-2:]
    count = len(shares) + 1
    shard = own_ref.shape[0] - FEAT_ROWS
    total = own_ref[:shard, :]
    for share in shares:
        total = total + share[:shard, :].astype(F32)
    out_ref[:shard, :] = total
    for d, share in enumerate((own_ref, *shares)):
        slot_ref[lax.rem(lax.axis_index("ctx") + (count - d), count)] = share[shard:, :].astype(F32)
    total = slot_ref[0]
    for d in range(1, count):
        total = total + slot_ref[d]
    out_ref[shard:, :] = total


def joined_kernel(mine_ref, other_ref, dfilt_ref, dfeat_ref):
    shard, width = dfilt_ref.shape[0], mine_ref.shape[1]
    here = pl.multiple_of(lax.axis_index("sub") * width, 128)
    there = pl.multiple_of((1 - lax.axis_index("sub")) * width, 128)
    for at, half in ((here, mine_ref), (there, other_ref)):
        dfilt_ref[:, pl.ds(at, width)] = half[:shard, :]
        for i in range(3):
            dfeat_ref[i, :, pl.ds(at, width)] = half[shard + 8 * i : shard + 8 * i + KF, :]


def local(streams, feat_taps, long_filter, upstream, score_dir, seg_lengths, list_ids):
    rows, chans = streams.shape[1:]
    segs = seg_lengths.shape[0]
    shard = long_filter.shape[0]
    ring = ("ctx", "sub")
    tokens = rows * lax.axis_size("ctx") * lax.axis_size("sub")
    shards = lax.axis_size("ctx")
    ahead, behind, own_wave, back = half_wave(rows)
    after = ahead[:, rows:]
    ahead, behind, own_wave, back, after = (jnp.asarray(t) for t in (ahead, behind, own_wave, back, after))
    direction = score_dir.reshape(1, chans)

    smem = pl.BlockSpec(memory_space=pltpu.SMEM)
    anywhere = pl.BlockSpec(memory_space=pl.ANY)
    here = pl.BlockSpec(memory_space=pltpu.VMEM)
    out = lambda dtype, *shape: jax.ShapeDtypeStruct(shape, dtype)
    vmem = lambda dtype, *shape: pltpu.VMEM(shape, dtype)
    shifts = vmem(BF, (KF - 1) * rows, rows + RIM)
    wide, tall, square = vmem(jnp.int32, 2 * rows, 2 * rows), vmem(jnp.int32, rows, 2 * rows), vmem(jnp.int32, 2 * rows, rows)

    def call(kernel, name, us, scalars, arrays, outs, scratch, **more):
        return pl.pallas_call(
            lambda *refs: kernel(*((tokens,) if scalars else ()), *refs),
            in_specs=[smem] * len(scalars) + [here] * len(arrays),
            out_specs=jax.tree.map(lambda _: here, outs), out_shape=outs, scratch_shapes=scratch,
            compiler_params=pltpu.CompilerParams(vmem_limit_bytes=VMEM_LIMIT),
            cost_estimate=pl.CostEstimate(flops=int(us * 1e9), bytes_accessed=int(us * 3e6), transcendentals=0),
            name=name, **more,
        )(*scalars, *arrays)

    sq, tails, part = pl.pallas_call(
        cut_kernel,
        in_specs=[anywhere, anywhere], out_specs=[anywhere] * 3,
        out_shape=[out(BF, rows, chans), out(BF, 3, RIM, chans), out(BF, shard, chans // 2)],
        scratch_shapes=[pltpu.SemaphoreType.DMA((3,))],
        compiler_params=pltpu.CompilerParams(vmem_limit_bytes=VMEM_LIMIT), name="cut",
    )(streams, long_filter)
    halo = passed_along(tails, ring, 1)
    gathered = [rotated(part, "ctx", d) for d in range(1, shards)]
    sq_next = passed_along(sq, ring, -1)

    query, key_feat, value_feat, product = call(
        feat_kernel, "feats", 4, [seg_lengths], [streams, halo, feat_taps], [out(BF, rows, chans)] * 4, [shifts])
    z_prev = passed_along(product, ring, 1)
    cross, a_own = call(
        spectra_kernel, "own_spectra", 5, [seg_lengths], [product, query, upstream, own_wave],
        [out(BF, segs, 2 * rows, chans), out(F32, 2 * rows, chans)], [square])

    gathered, sq_next, a_own = lax.optimization_barrier((gathered, sq_next, a_own))
    mine = jnp.stack([part] + gathered)
    other = swapped(mine, "sub", 1)
    up_held, _ = lax.optimization_barrier((upstream, mine))
    up_next = passed_along(up_held, ring, -1)

    q_next, spectrum, rim_cross, partial = call(
        score_kernel, "scores", 4, [seg_lengths],
        [streams, sq_next, feat_taps, mine, other, product, direction, cross, after, own_wave],
        [out(BF, rows, chans), out(F32, 2 * rows, chans), out(BF, 2 * rows, chans), out(F32, segs, 128)],
        [shifts, vmem(F32, LH, chans)])

    def dzq_of(held):
        return call(dzq_kernel, "adjoint_of_q", 4, [seg_lengths], [query, q_next, held, ahead, back],
                    out(F32, rows, chans), [wide, tall])

    def mixed_of(held):
        return call(w_kernel, "mixed", 4, [seg_lengths], [product, z_prev, held, behind, back],
                    out(F32, rows, chans), [wide, tall])

    def dzu_of(held):
        return call(dzu_kernel, "adjoint_of_up", 5, [seg_lengths],
                    [query, q_next, upstream, up_next, held, product, a_own, ahead, own_wave, back],
                    [out(F32, rows, chans), out(F32, 2 * rows, chans)], [wide, tall, vmem(BF, 2 * rows, chans)])

    waiting = [dzu_of, mixed_of, dzq_of]
    results = []
    totals = partial
    for axis in ("sub", "fsdp", "ctx"):
        distance = 1
        while distance < lax.axis_size(axis):
            arrived = swapped(totals, axis, distance)
            if axis != "sub" and waiting:
                arrived, result = lax.optimization_barrier((arrived, waiting.pop()(spectrum)))
                results.append(result)
            totals = totals + arrived
            distance *= 2
    results += [make(spectrum) for make in reversed(waiting)]
    dzq, mixed, (dzu, a_total) = results

    grads, heads, send, keep = call(
        grads_kernel, "gradients", 5, [seg_lengths, list_ids],
        [totals, streams, halo, query, key_feat, value_feat, upstream, direction,
         mixed, dzu, dzq, a_total, rim_cross, cross, back],
        [out(BF, 3, rows, chans), out(BF, 3, RIM, chans), out(BF, LH + FEAT_ROWS, chans // 2),
         out(F32, LH + FEAT_ROWS, chans // 2)],
        [shifts, vmem(F32, segs, 128), vmem(F32, rows, 128), vmem(F32, 2 * rows, chans)])
    received = swapped(send, "sub", 1)
    shares = call(
        shares_kernel, "shares", 1, [], [keep, received],
        [out(F32, shard + FEAT_ROWS, chans // 2)] + [out(BF, shard + FEAT_ROWS, chans // 2)] * (shards - 1), [])
    parts = [rotated(shares[d], "ctx", d) for d in range(1, shards)]
    rim = passed_along(heads, ring, -1)
    d_streams = call(
        dstreams_kernel, "stream_grads", 4, [seg_lengths], [grads, rim, feat_taps], out(BF, 3, rows, chans), [shifts])
    parts, d_streams = lax.optimization_barrier((parts, d_streams))
    summed = call(
        finish_kernel, "shard_sums", 1, [], [shares[0], *parts], out(F32, shard + FEAT_ROWS, chans // 2),
        [vmem(F32, shards, FEAT_ROWS, chans // 2)])
    d_filter, d_feat = call(
        joined_kernel, "both_halves", 1, [], [summed, swapped(summed, "sub", 1)],
        [out(F32, shard, chans), out(F32, 3, KF, chans)], [])
    return (d_streams, d_feat, d_filter)


def solution(mesh):
    placed = (
        P(None, ("groups", "ctx", "sub"), "fsdp"),
        P(None, None, "fsdp"),
        P("ctx", "fsdp"),
        P(("groups", "ctx", "sub"), "fsdp"),
        P("fsdp"),
        P("groups"),
        P("groups"),
    )
    return jax.shard_map(
        local,
        mesh=mesh,
        in_specs=placed,
        out_specs=(
            P(None, ("groups", "ctx", "sub"), "fsdp"),
            P("groups", None, "fsdp"),
            P(("groups", "ctx"), "fsdp"),
        ),
        check_vma=False,
    )
```

```python
import jax
import jax.numpy as jnp
import numpy as np
from jax import lax
from jax.experimental import pallas as pl
from jax.experimental.pallas import tpu as pltpu
from jax.sharding import PartitionSpec as P

LH = 128
KF = 7
RIM = 16
FEAT_ROWS = 24
BF = jnp.bfloat16
F32 = jnp.float32
VMEM_LIMIT = 16 * 1024 * 1024
TILE = 512


def passed_along(value, axis, steps):
    count = lax.axis_size(axis)
    leading, last = (max(0, -steps), min(count, count - steps))
    return lax.ppermute(value, axis, [(source, source + steps) for source in range(leading, last)])


def swapped(value, axis, distance):
    count = lax.axis_size(axis)
    return lax.ppermute(value, axis, [(source, source ^ distance) for source in range(count)])


def rotated(value, axis, distance):
    count = lax.axis_size(axis)
    return lax.ppermute(value, axis, [(source, (source + distance) % count) for source in range(count)])


def half_wave(rows):
    odd = 2 * np.arange(rows)[:, None] + 1
    span = np.arange(-rows, 2 * rows)[None, :]
    angle = np.pi * ((odd * span) % (4 * rows)) / (2 * rows)
    table = np.concatenate([np.cos(angle), -np.sin(angle)], axis=0)
    before, own, after = np.split(table, 3, axis=1)
    back = own.T / rows
    as_f32 = lambda parts: np.concatenate(parts, axis=1).astype(np.float32)
    return as_f32([own, after]), as_f32([own, before]), as_f32([own]), as_f32([back])


def dot(left, right):
    return jnp.dot(left, right, preferred_element_type=F32)


class Layout:
    def __init__(self, len_ref, rows, tokens):
        self.rows, self.tokens = rows, tokens
        self.count = len_ref.shape[0]
        self.base = (lax.axis_index("ctx") * lax.axis_size("sub") + lax.axis_index("sub")) * rows
        offset = jnp.int32(0)
        self.offsets = []
        for s in range(self.count):
            self.offsets.append(offset)
            offset = offset + len_ref[s]

    def segment(self, position):
        seg = jnp.zeros_like(position)
        for s in range(1, self.count):
            seg = seg + jnp.where(position >= self.offsets[s], 1, 0)
        return jnp.where((position >= 0) & (position < self.tokens), seg, -1)

    def age(self, position):
        start = jnp.zeros_like(position)
        for s in range(1, self.count):
            start = jnp.where(position >= self.offsets[s], self.offsets[s], start)
        return position - start

    def scalar_segment(self, position):
        seg = jnp.int32(0)
        for s in range(1, self.count):
            seg = seg + jnp.where(position >= self.offsets[s], 1, 0)
        return seg

    def span(self):
        return self.scalar_segment(self.base), self.scalar_segment(self.base + self.rows - 1) + 1


def tiles(chans):
    tile = min(TILE, chans)
    return [pl.ds(c, tile) for c in range(0, chans, tile)]


def causal_shifts(sm_ref, layout, first):
    rows = layout.rows
    row = lax.broadcasted_iota(jnp.int32, (rows, rows + RIM), 0)
    col = lax.broadcasted_iota(jnp.int32, (rows, rows + RIM), 1)
    age = layout.age(layout.base + first + row)
    for j in range(1, KF):
        hit = (col == row + (RIM - j)) & (age >= j)
        sm_ref[(j - 1) * rows : j * rows, :] = jnp.where(hit, 1.0, 0.0).astype(BF)


def reverse_shifts(sm_ref, layout):
    rows = layout.rows
    row = lax.broadcasted_iota(jnp.int32, (rows, rows + RIM), 0)
    col = lax.broadcasted_iota(jnp.int32, (rows, rows + RIM), 1)
    age = layout.age(layout.base + col)
    for j in range(1, KF):
        hit = (col == row + j) & (age >= j)
        sm_ref[(j - 1) * rows : j * rows, :] = jnp.where(hit, 1.0, 0.0).astype(BF)


def tap_sum(sm_ref, taps, here, x, rows):
    total = here.astype(F32) * taps[0:1, :]
    moved = dot(sm_ref[...], x)
    for j in range(1, KF):
        total = total + moved[(j - 1) * rows : j * rows] * taps[j : j + 1, :]
    return total


def cut_kernel(tokens, streams_ref, filter_ref, taps_ref, up_ref, len_ref, query_ref, tail_ref, half_ref,
               streams_out, taps_out, up_out, own_ref, next_ref, back_ref, ahead_ref, before_ref, rows_ref, held_ref, sems):
    rows = streams_ref.shape[1]
    width = half_ref.shape[1]
    at = pl.multiple_of(lax.axis_index("sub") * width, 128)
    pairs = [
        (len_ref, held_ref),
        (streams_ref.at[:, pl.ds(rows - RIM, RIM), :], tail_ref),
        (filter_ref.at[:, pl.ds(at, width)], half_ref),
        (streams_ref.at[0], query_ref),
        (streams_ref, streams_out),
        (taps_ref, taps_out),
        (up_ref, up_out),
    ]
    copies = [pltpu.make_async_copy(*pair, sems.at[n]) for n, pair in enumerate(pairs)]
    for copy in copies:
        copy.start()
    copies[0].wait()
    layout = Layout(held_ref, rows, tokens)
    causal_shifts(own_ref, layout, 0)
    causal_shifts(next_ref, layout, rows)
    reverse_shifts(back_ref, layout)
    ahead_ref[...] = segment_columns(layout, ahead_ref.shape, 0, rows)
    before_ref[...] = segment_columns(layout, before_ref.shape, -rows, 0)
    rows_ref[...] = segment_rows(layout, rows_ref.shape)
    for copy in copies[1:]:
        copy.wait()


def feat_kernel(s_ref, halo_ref, taps_ref, sm_ref, q_ref, k_ref, v_ref, z_ref):
    rows = s_ref.shape[1]
    for c in tiles(s_ref.shape[2]):
        feats = []
        for i, out in enumerate((q_ref, k_ref, v_ref)):
            here = s_ref[i, :, c]
            x = jnp.concatenate([halo_ref[i, :, c], here], axis=0)
            feat = tap_sum(sm_ref, taps_ref[i, :, c], here, x, rows).astype(BF)
            out[:, c] = feat
            feats.append(feat)
        z_ref[:, c] = (feats[1].astype(F32) * feats[2].astype(F32)).astype(BF)


def segment_columns(layout, shape, first_own, first_rim):
    rows = layout.rows
    col = lax.broadcasted_iota(jnp.int32, shape, 1)
    return layout.segment(layout.base + jnp.where(col < rows, col + first_own, col - rows + first_rim))


def segment_rows(layout, shape):
    return layout.segment(layout.base + lax.broadcasted_iota(jnp.int32, shape, 0))


def kept(table, seg_table, s):
    return jnp.where(seg_table == s, table, 0.0).astype(BF)


def times(a, b, rows):
    ar, ai, br, bi = a[:rows], a[rows:], b[:rows], b[rows:]
    return jnp.concatenate([ar * br - ai * bi, ar * bi + ai * br], axis=0)


def conj_times(a, b, rows):
    ar, ai, br, bi = a[:rows], a[rows:], b[:rows], b[rows:]
    return jnp.concatenate([ar * br + ai * bi, ar * bi - ai * br], axis=0)


def spectra_kernel(tokens, len_ref, z_ref, q_ref, own_ref, segc_ref, z_spec_ref, cross_ref, zs_ref, qs_ref):
    rows, chans = z_ref.shape
    layout = Layout(len_ref, rows, tokens)

    def one_segment(s, carry):
        wave = kept(own_ref[...], segc_ref[:, :rows], s)
        for c in tiles(chans):
            zs_ref[:, c] = dot(wave, z_ref[:, c])
            qs_ref[:, c] = dot(wave, q_ref[:, c])
        for c in tiles(chans):
            z_spec_ref[s, :, c] = zs_ref[:, c].astype(BF)
            cross_ref[s, :, c] = conj_times(zs_ref[:, c], qs_ref[:, c], rows).astype(BF)
        return carry

    lax.fori_loop(*layout.span(), one_segment, 0)


def score_kernel(tokens, len_ref, s_ref, sqn_ref, taps_ref, mine_ref, other_ref, dir_ref, z_spec_ref, cross_ref,
                 after_ref, own_ref, sm_ref, segc_ref, qn_ref, h_ref, rim_ref, part_ref, filt_ref, spec_ref):
    rows, chans = sqn_ref.shape
    layout = Layout(len_ref, rows, tokens)
    first, end = layout.span()
    own = own_ref[...].astype(BF)
    after = kept(after_ref[...], segc_ref[:, rows:], end - 1)
    part_ref[...] = jnp.zeros_like(part_ref)

    def add(s, c, cross):
        row = jnp.sum(h_ref[:, c] * cross, axis=0, keepdims=True) * dir_ref[:, c] * (1.0 / rows)
        lanes = row[:, :128]
        for n in range(128, row.shape[1], 128):
            lanes = lanes + row[:, n : n + 128]
        part_ref[pl.ds(s, 1), :] += lanes

    shards, shard, width = mine_ref.shape
    for ref, half in ((mine_ref, lax.axis_index("sub")), (other_ref, 1 - lax.axis_index("sub"))):
        at = pl.ds(pl.multiple_of(half * width, 128), width)
        for n in range(shards):
            row = jnp.bitwise_xor(lax.axis_index("ctx"), n) * shard
            filt_ref[pl.ds(pl.multiple_of(row, 8), shard), at] = ref[n].astype(F32)
    for c in tiles(chans):
        here = sqn_ref[:, c]
        x = jnp.concatenate([s_ref[0, rows - RIM :, c], here], axis=0)
        qn_ref[:, c] = tap_sum(sm_ref, taps_ref[0, :, c], here, x, rows).astype(BF)
    for c in tiles(chans):
        h_ref[:, c] = dot(own, filt_ref[:, c].astype(BF))
        spec_ref[:, c] = dot(after, qn_ref[:, c])
    for c in tiles(chans):
        spec = spec_ref[:, c]
        rim = conj_times(z_spec_ref[end - 1, :, c].astype(F32), spec, rows)
        rim_ref[:, c] = rim.astype(BF)
        add(end - 1, c, rim)

    def one_segment(s, carry):
        for c in tiles(chans):
            add(s, c, cross_ref[s, :, c].astype(F32))
        return carry

    lax.fori_loop(first, end, one_segment, 0)


def dzq_kernel(tokens, len_ref, q_ref, qn_ref, h_ref, ahead_ref, back_ref, segc_ref, segr_ref, dzq_ref, spec_ref, g_ref):
    rows, chans = q_ref.shape
    first, end = Layout(len_ref, rows, tokens).span()

    def one_segment(s, fresh):
        wave, back = kept(ahead_ref[...], segc_ref[...], s), kept(back_ref[...], segr_ref[...], s)
        for c in tiles(chans):
            spec_ref[:, c] = dot(wave, jnp.concatenate([q_ref[:, c], qn_ref[:, c]], axis=0))
        for c in tiles(chans):
            g_ref[:, c] = conj_times(h_ref[:, c], spec_ref[:, c], rows).astype(BF)
        for c in tiles(chans):
            term = dot(back, g_ref[:, c])
            dzq_ref[:, c] = term if fresh else dzq_ref[:, c] + term

    each_segment(first, end, one_segment)


def each_segment(first, end, one_segment):
    def inner(s, carry):
        one_segment(s, False)
        return carry

    one_segment(first, True)
    lax.fori_loop(first + 1, end, inner, 0)


def w_kernel(tokens, len_ref, z_spec_ref, zp_ref, h_ref, before_ref, back_ref, segb_ref, segr_ref, w_ref, g_ref, spec_ref):
    rows, chans = w_ref.shape
    first, end = Layout(len_ref, rows, tokens).span()
    before = kept(before_ref[...], segb_ref[...], first)
    for c in tiles(chans):
        spec_ref[:, c] = dot(before, zp_ref[:, c])

    def one_segment(s, fresh):
        back = kept(back_ref[...], segr_ref[...], s)
        for c in tiles(chans):
            spectrum = z_spec_ref[s, :, c].astype(F32)
            if fresh:
                spectrum = spectrum + spec_ref[:, c]
            g_ref[:, c] = times(h_ref[:, c], spectrum, rows).astype(BF)
        for c in tiles(chans):
            term = dot(back, g_ref[:, c])
            w_ref[:, c] = term if fresh else w_ref[:, c] + term

    each_segment(first, end, one_segment)


def dzu_kernel(tokens, len_ref, q_ref, qn_ref, up_ref, upn_ref, h_ref, z_spec_ref, ahead_ref, back_ref, segc_ref, segr_ref,
               dzu_ref, a_ref, u_ref, spec_ref, g_ref):
    rows, chans = q_ref.shape
    first, end = Layout(len_ref, rows, tokens).span()
    for c in tiles(chans):
        u_ref[:rows, c] = (q_ref[:, c].astype(F32) * up_ref[:, c].astype(F32)).astype(BF)
        u_ref[rows:, c] = (qn_ref[:, c].astype(F32) * upn_ref[:, c].astype(F32)).astype(BF)

    def one_segment(s, fresh):
        wave, back = kept(ahead_ref[...], segc_ref[...], s), kept(back_ref[...], segr_ref[...], s)
        for c in tiles(chans):
            spec_ref[:, c] = dot(wave, u_ref[:, c])
        for c in tiles(chans):
            spectrum = spec_ref[:, c]
            g_ref[:, c] = conj_times(h_ref[:, c], spectrum, rows).astype(BF)
            cross = conj_times(z_spec_ref[s, :, c].astype(F32), spectrum, rows)
            a_ref[:, c] = cross if fresh else a_ref[:, c] + cross
        for c in tiles(chans):
            term = dot(back, g_ref[:, c])
            dzu_ref[:, c] = term if fresh else dzu_ref[:, c] + term

    each_segment(first, end, one_segment)


def coefficients(len_ref, ids_ref, part_ref):
    count = len_ref.shape[0]
    index = lax.broadcasted_iota(jnp.int32, (count, 128), 0)
    length = jnp.zeros((count, 128), F32)
    ids = jnp.zeros((count, 128), jnp.int32)
    for s in range(count):
        length = jnp.where(index == s, len_ref[s].astype(F32), length)
        ids = jnp.where(index == s, ids_ref[s], ids)
    scores = jnp.broadcast_to(jnp.sum(part_ref[...], axis=1, keepdims=True), (count, 128)) / length
    total = jnp.zeros((count, 128), F32)
    mates = jnp.zeros((count, 128), F32)
    for s in range(count):
        same = jnp.where(ids == ids_ref[s], 1.0, 0.0)
        mates = mates + same
        total = total + same * scores[s : s + 1, :]
    return (scores - total / mates) / length


def token_coefficients(coef, seg):
    spread = jnp.zeros(seg.shape, F32)
    for s in range(coef.shape[0]):
        spread = jnp.where(seg == s, coef[s : s + 1, :], spread)
    return spread


def across(column, width):
    return jnp.concatenate([column] * (width // 128), axis=1)


def grads_kernel(tokens, len_ref, ids_ref, part_ref, q_ref, k_ref, v_ref, up_ref, dir_ref, w_ref, dzu_ref, dzq_ref,
                 da_ref, head_ref, coef_ref, tok_ref):
    rows, chans = q_ref.shape
    layout = Layout(len_ref, rows, tokens)
    coef = coefficients(len_ref, ids_ref, part_ref)
    coef_ref[...] = coef
    tok_ref[...] = token_coefficients(coef, segment_rows(layout, (rows, 128)))
    for c in tiles(chans):
        rise = across(tok_ref[...], c.size) * dir_ref[:, c]
        dz = dzu_ref[:, c] + rise * dzq_ref[:, c]
        dq = ((up_ref[:, c].astype(F32) + rise) * w_ref[:, c]).astype(BF)
        dk = (dz * v_ref[:, c].astype(F32)).astype(BF)
        dv = (dz * k_ref[:, c].astype(F32)).astype(BF)
        for i, da in enumerate((dq, dk, dv)):
            da_ref[i, :, c] = da
            head_ref[i, :, c] = da[:RIM]


def weights_kernel(tokens, mine, len_ref, coef_ref, s_ref, halo_ref, da_ref, dir_ref, a_ref, rim_ref, cross_ref, back_ref,
                   sm_ref, out_ref, acc_ref):
    rows = da_ref.shape[1]
    width = out_ref.shape[1]
    layout = Layout(len_ref, rows, tokens)
    first, end = layout.span()
    half = lax.axis_index("sub") if mine else 1 - lax.axis_index("sub")
    spans = [(c, pl.ds(pl.multiple_of(half * width + c.start, 128), c.size)) for c in tiles(width)]

    def weight(s, at):
        return across(coef_ref[pl.ds(s, 1), :], at.size) * dir_ref[:, at]

    for c, at in spans:
        acc_ref[:, c] = a_ref[:, at] + weight(end - 1, at) * rim_ref[:, at].astype(F32)

    def one_segment(s, carry):
        for c, at in spans:
            acc_ref[:, c] += weight(s, at) * cross_ref[s, :, at].astype(F32)
        return carry

    lax.fori_loop(first, end, one_segment, 0)
    for c, at in spans:
        blocks = [dot(back_ref[...].astype(BF), acc_ref[:, c].astype(BF))]
        for i in range(3):
            grad = da_ref[i, :, at].astype(F32)
            here = s_ref[i, :, at]
            moved = dot(sm_ref[...], jnp.concatenate([halo_ref[i, :, at], here], axis=0))
            sums = [jnp.sum(grad * here.astype(F32), axis=0, keepdims=True)]
            for j in range(1, KF):
                sums.append(jnp.sum(grad * moved[(j - 1) * rows : j * rows], axis=0, keepdims=True))
            sums.append(jnp.zeros_like(sums[0]))
            blocks.append(jnp.concatenate(sums, axis=0))
        out_ref[:, c] = jnp.concatenate(blocks, axis=0).astype(out_ref.dtype)


def dstreams_kernel(da_ref, rim_ref, taps_ref, sm_ref, out_ref):
    rows, chans = da_ref.shape[1:]
    for c in tiles(chans):
        for i in range(3):
            here = da_ref[i, :, c]
            x = jnp.concatenate([here, rim_ref[i, :, c]], axis=0)
            out_ref[i, :, c] = tap_sum(sm_ref, taps_ref[i, :, c], here, x, rows).astype(BF)


def shares_kernel(keep_ref, recv_ref, own_ref, *share_refs):
    count = len(share_refs) + 1
    shard = own_ref.shape[0] - FEAT_ROWS
    taps = keep_ref.shape[0] - FEAT_ROWS
    feat = (keep_ref[taps:, :] + recv_ref[taps:, :].astype(F32)).astype(BF)
    for d in range(count):
        at = pl.ds(pl.multiple_of(lax.rem(lax.axis_index("ctx") + d, count) * shard, 8), shard)
        total = keep_ref[at, :] + recv_ref[at, :].astype(F32)
        ref = own_ref if d == 0 else share_refs[d - 1]
        ref[:shard, :] = total.astype(ref.dtype)
        ref[shard:, :] = feat.astype(ref.dtype)


def finish_kernel(own_ref, *refs):
    shares, (out_ref, slot_ref) = refs[:-2], refs[-2:]
    count = len(shares) + 1
    shard = own_ref.shape[0] - FEAT_ROWS
    total = own_ref[:shard, :]
    for share in shares:
        total = total + share[:shard, :].astype(F32)
    out_ref[:shard, :] = total
    for d, share in enumerate((own_ref, *shares)):
        slot_ref[lax.rem(lax.axis_index("ctx") + (count - d), count)] = share[shard:, :].astype(F32)
    total = slot_ref[0]
    for d in range(1, count):
        total = total + slot_ref[d]
    out_ref[shard:, :] = total


def joined_kernel(mine_ref, other_ref, dfilt_ref, dfeat_ref):
    shard, width = dfilt_ref.shape[0], mine_ref.shape[1]
    here = pl.multiple_of(lax.axis_index("sub") * width, 128)
    there = pl.multiple_of((1 - lax.axis_index("sub")) * width, 128)
    for at, half in ((here, mine_ref), (there, other_ref)):
        dfilt_ref[:, pl.ds(at, width)] = half[:shard, :]
        for i in range(3):
            dfeat_ref[i, :, pl.ds(at, width)] = half[shard + 8 * i : shard + 8 * i + KF, :]


def local(streams, feat_taps, long_filter, upstream, score_dir, seg_lengths, list_ids):
    rows, chans = streams.shape[1:]
    segs = seg_lengths.shape[0]
    shard = long_filter.shape[0]
    ring = ("ctx", "sub")
    tokens = rows * lax.axis_size("ctx") * lax.axis_size("sub")
    shards = lax.axis_size("ctx")
    ahead, behind, own_wave, back = half_wave(rows)
    after, before = ahead[:, rows:], behind[:, rows:]
    ahead, own_wave, back, after, before = (jnp.asarray(t) for t in (ahead, own_wave, back, after, before))
    direction = score_dir.reshape(1, chans)

    smem = pl.BlockSpec(memory_space=pltpu.SMEM)
    anywhere = pl.BlockSpec(memory_space=pl.ANY)
    here = pl.BlockSpec(memory_space=pltpu.VMEM)
    out = lambda dtype, *shape: jax.ShapeDtypeStruct(shape, dtype)
    vmem = lambda dtype, *shape: pltpu.VMEM(shape, dtype)
    def call(kernel, name, us, scalars, arrays, outs, scratch, **more):
        return pl.pallas_call(
            lambda *refs: kernel(*((tokens,) if scalars else ()), *refs),
            in_specs=[smem] * len(scalars) + [here] * len(arrays),
            out_specs=jax.tree.map(lambda _: here, outs), out_shape=outs, scratch_shapes=scratch,
            compiler_params=pltpu.CompilerParams(vmem_limit_bytes=VMEM_LIMIT),
            cost_estimate=pl.CostEstimate(flops=int(us * 1e7), bytes_accessed=int(us * 3e4), transcendentals=0),
            name=name, **more,
        )(*scalars, *arrays)

    in_hbm = pl.BlockSpec(memory_space=pltpu.HBM)
    shifts = out(BF, (KF - 1) * rows, rows + RIM)
    table = lambda *shape: out(jnp.int32, *shape)
    (sq, tails, part, streams, feat_taps, upstream, own_shifts, next_shifts, back_shifts,
     seg_ahead, seg_before, seg_rows) = pl.pallas_call(
        lambda *refs: cut_kernel(tokens, *refs),
        in_specs=[in_hbm] * 5, out_specs=[here] * 12,
        out_shape=[out(BF, rows, chans), out(BF, 3, RIM, chans), out(BF, shard, chans // 2),
                   out(BF, *streams.shape), out(F32, *feat_taps.shape), out(BF, *upstream.shape),
                   shifts, shifts, shifts, table(2 * rows, 2 * rows), table(2 * rows, rows), table(rows, 2 * rows)],
        scratch_shapes=[pltpu.SMEM((segs,), jnp.int32), pltpu.SemaphoreType.DMA((7,))],
        compiler_params=pltpu.CompilerParams(vmem_limit_bytes=VMEM_LIMIT), name="cut",
    )(*(pltpu.with_memory_space_constraint(x, pltpu.HBM)
        for x in (streams, long_filter, feat_taps, upstream, seg_lengths)))
    sq_next = passed_along(sq, ring, -1)
    held, order = part[None], [0]
    distance = shards // 2
    if distance:
        held = jnp.concatenate([held, swapped(held, "ctx", distance)], axis=0)
        order = [0, distance]
    halo = passed_along(tails, ring, 1)
    held, halo = lax.optimization_barrier((held, halo))
    distance //= 2
    while distance:
        held = jnp.concatenate([held, swapped(held, "ctx", distance)], axis=0)
        order = order + [n ^ distance for n in order]
        distance //= 2
    mine = jnp.stack([held[order.index(n)] for n in range(shards)])

    query, key_feat, value_feat, product = call(
        feat_kernel, "feats", 4, [], [streams, halo, feat_taps, own_shifts], [out(BF, rows, chans)] * 4, [])
    z_prev = passed_along(product, ring, 1)
    one_spectrum, one_product = vmem(F32, 2 * rows, chans), vmem(BF, 2 * rows, chans)
    spectra = out(BF, segs, 2 * rows, chans)
    z_spec, cross = call(
        spectra_kernel, "own_spectra", 4, [seg_lengths], [product, query, own_wave, seg_ahead],
        [spectra] * 2, [one_spectrum, one_spectrum])

    mine, z_spec = lax.optimization_barrier((mine, z_spec))
    other = swapped(mine, "sub", 1)

    q_next, spectrum, rim_cross, partial = call(
        score_kernel, "scores", 4, [seg_lengths],
        [streams, sq_next, feat_taps, mine, other, direction, z_spec, cross, after, own_wave, next_shifts, seg_ahead],
        [out(BF, rows, chans), out(F32, 2 * rows, chans), out(BF, 2 * rows, chans),
         out(F32, segs, 128)],
        [vmem(F32, LH, chans), one_spectrum])
    up_held, partial = lax.optimization_barrier((upstream, partial))
    up_next = passed_along(up_held, ring, -1)

    def dzq_of(held):
        return call(dzq_kernel, "adjoint_of_q", 4, [seg_lengths], [query, q_next, held, ahead, back, seg_ahead, seg_rows],
                    out(F32, rows, chans), [one_spectrum, one_product])

    def mixed_of(held):
        return call(w_kernel, "mixed", 4, [seg_lengths], [z_spec, z_prev, held, before, back, seg_before, seg_rows],
                    out(F32, rows, chans), [one_product, one_spectrum])

    def dzu_of(held):
        return call(dzu_kernel, "adjoint_of_up", 5, [seg_lengths],
                    [query, q_next, upstream, up_next, held, z_spec, ahead, back, seg_ahead, seg_rows],
                    [out(F32, rows, chans), out(F32, 2 * rows, chans)],
                    [one_product, one_spectrum, one_product])

    waiting = [dzu_of, dzq_of, mixed_of]
    results = []
    totals = partial
    for axis in ("sub", "fsdp", "ctx"):
        distance = 1
        while distance < lax.axis_size(axis):
            arrived = swapped(totals, axis, distance)
            if axis != "sub" and waiting:
                arrived, result = lax.optimization_barrier((arrived, waiting.pop()(spectrum)))
                results.append(result)
            totals = totals + arrived
            distance *= 2
    results += [make(spectrum) for make in reversed(waiting)]
    mixed, dzq, (dzu, a_total) = results

    grads, heads, coef = call(
        grads_kernel, "gradients", 2, [seg_lengths, list_ids],
        [totals, query, key_feat, value_feat, upstream, direction, mixed, dzu, dzq],
        [out(BF, 3, rows, chans), out(BF, 3, RIM, chans), out(F32, segs, 128)], [vmem(F32, rows, 128)])
    rim = passed_along(heads, ring, -1)
    def weights_of(mine, dtype, grads):
        return call(lambda tokens, *refs: weights_kernel(tokens, mine, *refs), "weight_grads", 2, [seg_lengths],
                    [coef, streams, halo, grads, direction, a_total, rim_cross, cross, back, own_shifts],
                    out(dtype, LH + FEAT_ROWS, chans // 2), [vmem(F32, 2 * rows, chans // 2)])

    send = weights_of(False, BF, grads)
    received = swapped(send, "sub", 1)
    grads, send = lax.optimization_barrier((grads, send))
    keep = weights_of(True, F32, grads)
    keep, rim = lax.optimization_barrier((keep, rim))
    shares = call(
        shares_kernel, "shares", 1, [], [keep, received],
        [out(F32, shard + FEAT_ROWS, chans // 2)] + [out(BF, shard + FEAT_ROWS, chans // 2)] * (shards - 1), [])
    parts = [rotated(shares[d], "ctx", d) for d in range(1, shards)]
    d_streams = call(
        dstreams_kernel, "stream_grads", 4, [], [grads, rim, feat_taps, back_shifts], out(BF, 3, rows, chans), [])
    parts, d_streams = lax.optimization_barrier((parts, d_streams))
    summed = call(
        finish_kernel, "shard_sums", 1, [], [shares[0], *parts], out(F32, shard + FEAT_ROWS, chans // 2),
        [vmem(F32, shards, FEAT_ROWS, chans // 2)])
    d_filter, d_feat = call(
        joined_kernel, "both_halves", 1, [], [summed, swapped(summed, "sub", 1)],
        [out(F32, shard, chans), out(F32, 3, KF, chans)], [])
    return (d_streams, d_feat, d_filter)


def solution(mesh):
    placed = (
        P(None, ("groups", "ctx", "sub"), "fsdp"),
        P(None, None, "fsdp"),
        P("ctx", "fsdp"),
        P(("groups", "ctx", "sub"), "fsdp"),
        P("fsdp"),
        P("groups"),
        P("groups"),
    )
    return jax.shard_map(
        local,
        mesh=mesh,
        in_specs=placed,
        out_specs=(
            P(None, ("groups", "ctx", "sub"), "fsdp"),
            P("groups", None, "fsdp"),
            P(("groups", "ctx"), "fsdp"),
        ),
        check_vma=False,
    )
```

```python
import jax
import jax.numpy as jnp
import numpy as np
from jax import lax
from jax.experimental import pallas as pl
from jax.experimental.pallas import tpu as pltpu
from jax.sharding import PartitionSpec as P

LH = 128
KF = 7
RIM = 16
FEAT_ROWS = 24
KEPT = 2
BF = jnp.bfloat16
F32 = jnp.float32
VMEM_LIMIT = 7 * 1024 * 1024
TILE = 512


def passed_along(value, axis, steps):
    count = lax.axis_size(axis)
    leading, last = (max(0, -steps), min(count, count - steps))
    return lax.ppermute(value, axis, [(source, source + steps) for source in range(leading, last)])


def swapped(value, axis, distance):
    count = lax.axis_size(axis)
    return lax.ppermute(value, axis, [(source, source ^ distance) for source in range(count)])


def rotated(value, axis, distance):
    count = lax.axis_size(axis)
    return lax.ppermute(value, axis, [(source, (source + distance) % count) for source in range(count)])


def half_wave(rows):
    odd = 2 * np.arange(rows)[:, None] + 1
    span = np.arange(-rows, 2 * rows)[None, :]
    angle = np.pi * ((odd * span) % (4 * rows)) / (2 * rows)
    table = np.concatenate([np.cos(angle), -np.sin(angle)], axis=0)
    before, own, after = np.split(table, 3, axis=1)
    back = own.T / rows
    as_f32 = lambda parts: np.concatenate(parts, axis=1).astype(np.float32)
    return as_f32([own, after]), as_f32([own, before]), as_f32([own]), as_f32([back])


def dot(left, right):
    return jnp.dot(left, right, preferred_element_type=F32)


class Layout:
    def __init__(self, len_ref, rows, tokens):
        self.rows, self.tokens = rows, tokens
        self.count = len_ref.shape[0]
        self.base = (lax.axis_index("ctx") * lax.axis_size("sub") + lax.axis_index("sub")) * rows
        offset = jnp.int32(0)
        self.offsets = []
        for s in range(self.count):
            self.offsets.append(offset)
            offset = offset + len_ref[s]

    def segment(self, position):
        seg = jnp.zeros_like(position)
        for s in range(1, self.count):
            seg = seg + jnp.where(position >= self.offsets[s], 1, 0)
        return jnp.where((position >= 0) & (position < self.tokens), seg, -1)

    def age(self, position):
        start = jnp.zeros_like(position)
        for s in range(1, self.count):
            start = jnp.where(position >= self.offsets[s], self.offsets[s], start)
        return position - start

    def scalar_segment(self, position):
        seg = jnp.int32(0)
        for s in range(1, self.count):
            seg = seg + jnp.where(position >= self.offsets[s], 1, 0)
        return seg

    def span(self):
        return self.scalar_segment(self.base), self.scalar_segment(self.base + self.rows - 1) + 1


def tiles(chans):
    tile = min(TILE, chans)
    return [pl.ds(c, tile) for c in range(0, chans, tile)]


def causal_shifts(sm_ref, layout, first):
    rows = layout.rows
    row = lax.broadcasted_iota(jnp.int32, (rows, rows + RIM), 0)
    col = lax.broadcasted_iota(jnp.int32, (rows, rows + RIM), 1)
    age = layout.age(layout.base + first + row)
    for j in range(1, KF):
        hit = (col == row + (RIM - j)) & (age >= j)
        sm_ref[(j - 1) * rows : j * rows, :] = jnp.where(hit, 1.0, 0.0).astype(BF)


def reverse_shifts(sm_ref, layout):
    rows = layout.rows
    row = lax.broadcasted_iota(jnp.int32, (rows, rows + RIM), 0)
    col = lax.broadcasted_iota(jnp.int32, (rows, rows + RIM), 1)
    age = layout.age(layout.base + col)
    for j in range(1, KF):
        hit = (col == row + j) & (age >= j)
        sm_ref[(j - 1) * rows : j * rows, :] = jnp.where(hit, 1.0, 0.0).astype(BF)


def tap_sum(sm_ref, taps, here, x, rows, keep=None):
    total = here.astype(F32) * taps[0:1, :]
    moved = dot(sm_ref[...], x)
    for j in range(1, KF):
        total = total + moved[(j - 1) * rows : j * rows] * taps[j : j + 1, :]
    if keep is not None:
        keep(moved.astype(BF))
    return total


def cut_kernel(tokens, streams_ref, filter_ref, taps_ref, up_ref, len_ref, query_ref, tail_ref, half_ref,
               streams_out, taps_out, up_out, own_ref, next_ref, back_ref, ahead_ref, before_ref, rows_ref, held_ref, sems):
    rows = streams_ref.shape[1]
    width = half_ref.shape[1]
    at = pl.multiple_of(lax.axis_index("sub") * width, 128)
    pairs = [
        (len_ref, held_ref),
        (streams_ref.at[:, pl.ds(rows - RIM, RIM), :], tail_ref),
        (filter_ref.at[:, pl.ds(at, width)], half_ref),
        (streams_ref.at[0], query_ref),
        (streams_ref, streams_out),
        (taps_ref, taps_out),
        (up_ref, up_out),
    ]
    copies = [pltpu.make_async_copy(*pair, sems.at[n]) for n, pair in enumerate(pairs)]
    for copy in copies:
        copy.start()
    copies[0].wait()
    layout = Layout(held_ref, rows, tokens)
    causal_shifts(own_ref, layout, 0)
    causal_shifts(next_ref, layout, rows)
    reverse_shifts(back_ref, layout)
    ahead_ref[...] = segment_columns(layout, ahead_ref.shape, 0, rows)
    before_ref[...] = segment_columns(layout, before_ref.shape, -rows, 0)
    rows_ref[...] = segment_rows(layout, rows_ref.shape)
    for copy in copies[1:]:
        copy.wait()


def feat_kernel(s_ref, halo_ref, taps_ref, sm_ref, q_ref, k_ref, v_ref, z_ref, moved_ref):
    rows = s_ref.shape[1]
    for c in tiles(s_ref.shape[2]):
        feats = []
        for i, out in enumerate((q_ref, k_ref, v_ref)):
            here = s_ref[i, :, c]
            x = jnp.concatenate([halo_ref[i, :, c], here], axis=0)

            def keep(moved):
                moved_ref[i - (3 - KEPT), :, c] = moved

            feat = tap_sum(sm_ref, taps_ref[i, :, c], here, x, rows, keep if i >= 3 - KEPT else None).astype(BF)
            out[:, c] = feat
            feats.append(feat)
        z_ref[:, c] = (feats[1].astype(F32) * feats[2].astype(F32)).astype(BF)


def segment_columns(layout, shape, first_own, first_rim):
    rows = layout.rows
    col = lax.broadcasted_iota(jnp.int32, shape, 1)
    return layout.segment(layout.base + jnp.where(col < rows, col + first_own, col - rows + first_rim))


def segment_rows(layout, shape):
    return layout.segment(layout.base + lax.broadcasted_iota(jnp.int32, shape, 0))


def kept(table, seg_table, s):
    return jnp.where(seg_table == s, table, 0.0).astype(BF)


def times(a, b, rows):
    ar, ai, br, bi = a[:rows], a[rows:], b[:rows], b[rows:]
    return jnp.concatenate([ar * br - ai * bi, ar * bi + ai * br], axis=0)


def conj_times(a, b, rows):
    ar, ai, br, bi = a[:rows], a[rows:], b[:rows], b[rows:]
    return jnp.concatenate([ar * br + ai * bi, ar * bi - ai * br], axis=0)


def spectra_kernel(tokens, len_ref, z_ref, q_ref, own_ref, segc_ref, z_spec_ref, q_spec_ref, cross_ref, zs_ref, qs_ref):
    rows, chans = z_ref.shape
    layout = Layout(len_ref, rows, tokens)

    def one_segment(s, carry):
        wave = kept(own_ref[...], segc_ref[:, :rows], s)
        for c in tiles(chans):
            zs_ref[:, c] = dot(wave, z_ref[:, c])
            qs_ref[:, c] = dot(wave, q_ref[:, c])
        for c in tiles(chans):
            z_spec_ref[s, :, c] = zs_ref[:, c].astype(BF)
            q_spec_ref[s, :, c] = qs_ref[:, c].astype(BF)
            cross_ref[s, :, c] = conj_times(zs_ref[:, c], qs_ref[:, c], rows).astype(BF)
        return carry

    lax.fori_loop(*layout.span(), one_segment, 0)


def score_kernel(tokens, len_ref, s_ref, sqn_ref, taps_ref, mine_ref, other_ref, dir_ref, z_spec_ref, cross_ref,
                 after_ref, own_ref, sm_ref, segc_ref, qn_ref, qn_spec_ref, h_ref, rim_ref, part_ref, filt_ref, spec_ref):
    rows, chans = sqn_ref.shape
    layout = Layout(len_ref, rows, tokens)
    first, end = layout.span()
    own = own_ref[...].astype(BF)
    after = kept(after_ref[...], segc_ref[:, rows:], end - 1)
    part_ref[...] = jnp.zeros_like(part_ref)

    def add(s, c, cross):
        row = jnp.sum(h_ref[:, c] * cross, axis=0, keepdims=True) * dir_ref[:, c] * (1.0 / rows)
        lanes = row[:, :128]
        for n in range(128, row.shape[1], 128):
            lanes = lanes + row[:, n : n + 128]
        part_ref[pl.ds(s, 1), :] += lanes

    shards, shard, width = mine_ref.shape
    for ref, half in ((mine_ref, lax.axis_index("sub")), (other_ref, 1 - lax.axis_index("sub"))):
        at = pl.ds(pl.multiple_of(half * width, 128), width)
        for n in range(shards):
            row = jnp.bitwise_xor(lax.axis_index("ctx"), n) * shard
            filt_ref[pl.ds(pl.multiple_of(row, 8), shard), at] = ref[n].astype(F32)
    for c in tiles(chans):
        here = sqn_ref[:, c]
        x = jnp.concatenate([s_ref[0, rows - RIM :, c], here], axis=0)
        qn_ref[:, c] = tap_sum(sm_ref, taps_ref[0, :, c], here, x, rows).astype(BF)
    for c in tiles(chans):
        h_ref[:, c] = dot(own, filt_ref[:, c].astype(BF))
        spec_ref[:, c] = dot(after, qn_ref[:, c])
    for c in tiles(chans):
        spec = spec_ref[:, c]
        qn_spec_ref[:, c] = spec.astype(BF)
        rim = conj_times(z_spec_ref[end - 1, :, c].astype(F32), spec, rows)
        rim_ref[:, c] = rim.astype(BF)
        add(end - 1, c, rim)

    def one_segment(s, carry):
        for c in tiles(chans):
            add(s, c, cross_ref[s, :, c].astype(F32))
        return carry

    lax.fori_loop(first, end, one_segment, 0)


def each_segment(first, end, one_segment):
    def inner(s, carry):
        one_segment(s, False)
        return carry

    one_segment(first, True)
    lax.fori_loop(first + 1, end, inner, 0)


def w_kernel(tokens, len_ref, z_spec_ref, zp_ref, h_ref, before_ref, back_ref, segb_ref, segr_ref, w_ref, g_ref, spec_ref):
    rows, chans = w_ref.shape
    first, end = Layout(len_ref, rows, tokens).span()
    before = kept(before_ref[...], segb_ref[...], first)
    for c in tiles(chans):
        spec_ref[:, c] = dot(before, zp_ref[:, c])

    def one_segment(s, fresh):
        back = kept(back_ref[...], segr_ref[...], s)
        for c in tiles(chans):
            spectrum = z_spec_ref[s, :, c].astype(F32)
            if fresh:
                spectrum = spectrum + spec_ref[:, c]
            g_ref[:, c] = times(h_ref[:, c], spectrum, rows).astype(BF)
        for c in tiles(chans):
            term = dot(back, g_ref[:, c])
            w_ref[:, c] = term if fresh else w_ref[:, c] + term

    each_segment(first, end, one_segment)


def u_kernel(tokens, len_ref, q_ref, qn_ref, up_ref, upn_ref, z_spec_ref, ahead_ref, segc_ref,
             u_spec_ref, a_ref, u_ref, spec_ref):
    rows, chans = q_ref.shape
    first, end = Layout(len_ref, rows, tokens).span()
    for c in tiles(chans):
        u_ref[:rows, c] = (q_ref[:, c].astype(F32) * up_ref[:, c].astype(F32)).astype(BF)
        u_ref[rows:, c] = (qn_ref[:, c].astype(F32) * upn_ref[:, c].astype(F32)).astype(BF)

    def one_segment(s, fresh):
        wave = kept(ahead_ref[...], segc_ref[...], s)
        for c in tiles(chans):
            spec_ref[:, c] = dot(wave, u_ref[:, c])
        for c in tiles(chans):
            spectrum = spec_ref[:, c]
            cross = conj_times(z_spec_ref[s, :, c].astype(F32), spectrum, rows)
            a_ref[:, c] = cross if fresh else a_ref[:, c] + cross
            u_spec_ref[s, :, c] = spectrum.astype(BF)

    each_segment(first, end, one_segment)


def coefficients(len_ref, ids_ref, part_ref):
    count = len_ref.shape[0]
    index = lax.broadcasted_iota(jnp.int32, (count, 128), 0)
    length = jnp.zeros((count, 128), F32)
    ids = jnp.zeros((count, 128), jnp.int32)
    for s in range(count):
        length = jnp.where(index == s, len_ref[s].astype(F32), length)
        ids = jnp.where(index == s, ids_ref[s], ids)
    scores = jnp.broadcast_to(jnp.sum(part_ref[...], axis=1, keepdims=True), (count, 128)) / length
    total = jnp.zeros((count, 128), F32)
    mates = jnp.zeros((count, 128), F32)
    for s in range(count):
        same = jnp.where(ids == ids_ref[s], 1.0, 0.0)
        mates = mates + same
        total = total + same * scores[s : s + 1, :]
    return (scores - total / mates) / length


def token_coefficients(coef, seg):
    spread = jnp.zeros(seg.shape, F32)
    for s in range(coef.shape[0]):
        spread = jnp.where(seg == s, coef[s : s + 1, :], spread)
    return spread


def across(column, width):
    return jnp.concatenate([column] * (width // 128), axis=1)


def grads_kernel(tokens, len_ref, ids_ref, part_ref, q_ref, k_ref, v_ref, up_ref, dir_ref, w_ref, h_ref,
                 u_spec_ref, q_spec_ref, qn_spec_ref, back_ref, segr_ref,
                 da_ref, head_ref, coef_ref, tok_ref, dz_ref, g_ref):
    rows, chans = q_ref.shape
    layout = Layout(len_ref, rows, tokens)
    first, end = layout.span()
    coef = coefficients(len_ref, ids_ref, part_ref)
    coef_ref[...] = coef
    tok_ref[...] = token_coefficients(coef, segment_rows(layout, (rows, 128)))
    dz_ref[...] = jnp.zeros_like(dz_ref)

    def one_segment(s, rim):
        back = kept(back_ref[...], segr_ref[...], s)
        for c in tiles(chans):
            weight = across(coef_ref[pl.ds(s, 1), :], c.size) * dir_ref[:, c]
            spectrum = q_spec_ref[s, :, c].astype(F32)
            if rim:
                spectrum = spectrum + qn_spec_ref[:, c].astype(F32)
            spectrum = u_spec_ref[s, :, c].astype(F32) + weight * spectrum
            g_ref[:, c] = conj_times(h_ref[:, c], spectrum, rows).astype(BF)
        for c in tiles(chans):
            dz_ref[:, c] += dot(back, g_ref[:, c])

    def inner(s, carry):
        one_segment(s, False)
        return carry

    lax.fori_loop(first, end - 1, inner, 0)
    one_segment(end - 1, True)
    for c in tiles(chans):
        rise = across(tok_ref[...], c.size) * dir_ref[:, c]
        dz = dz_ref[:, c]
        dq = ((up_ref[:, c].astype(F32) + rise) * w_ref[:, c]).astype(BF)
        dk = (dz * v_ref[:, c].astype(F32)).astype(BF)
        dv = (dz * k_ref[:, c].astype(F32)).astype(BF)
        for i, da in enumerate((dq, dk, dv)):
            da_ref[i, :, c] = da
            head_ref[i, :, c] = da[:RIM]


def weights_kernel(tokens, mine, len_ref, coef_ref, s_ref, halo_ref, moved_ref, da_ref, dir_ref, a_ref, rim_ref, cross_ref, back_ref,
                   sm_ref, out_ref, acc_ref):
    rows = da_ref.shape[1]
    width = out_ref.shape[1]
    layout = Layout(len_ref, rows, tokens)
    first, end = layout.span()
    block = lax.broadcasted_iota(jnp.int32, (16, KF * rows), 1) - rows * lax.broadcasted_iota(jnp.int32, (16, KF * rows), 0)
    sums = jnp.where((block >= 0) & (block < rows), 1.0, 0.0).astype(BF)
    half = lax.axis_index("sub") if mine else 1 - lax.axis_index("sub")
    spans = [(c, pl.ds(pl.multiple_of(half * width + c.start, 128), c.size)) for c in tiles(width)]

    def weight(s, at):
        return across(coef_ref[pl.ds(s, 1), :], at.size) * dir_ref[:, at]

    for c, at in spans:
        acc_ref[:, c] = a_ref[:, at] + weight(end - 1, at) * rim_ref[:, at].astype(F32)

    def one_segment(s, carry):
        for c, at in spans:
            acc_ref[:, c] += weight(s, at) * cross_ref[s, :, at].astype(F32)
        return carry

    lax.fori_loop(first, end, one_segment, 0)
    for c, at in spans:
        blocks = [dot(back_ref[...].astype(BF), acc_ref[:, c].astype(BF))]
        for i in range(3):
            here = s_ref[i, :, at]
            if i < 3 - KEPT:
                moved = dot(sm_ref[...], jnp.concatenate([halo_ref[i, :, at], here], axis=0))
                grad = da_ref[i, :, at].astype(F32)
                rows_of = [jnp.sum(grad * here.astype(F32), axis=0, keepdims=True)]
                for j in range(1, KF):
                    rows_of.append(jnp.sum(grad * moved[(j - 1) * rows : j * rows], axis=0, keepdims=True))
                blocks.append(jnp.concatenate(rows_of + [jnp.zeros_like(rows_of[0])], axis=0))
            else:
                grad = da_ref[i, :, at]
                moved = [here] + [moved_ref[i - (3 - KEPT), j * rows : (j + 1) * rows, at] for j in range(KF - 1)]
                blocks.append(dot(sums, jnp.concatenate([grad * x for x in moved], axis=0))[:8])
        out_ref[:, c] = jnp.concatenate(blocks, axis=0).astype(out_ref.dtype)


def dstreams_kernel(da_ref, rim_ref, taps_ref, sm_ref, out_ref):
    rows, chans = da_ref.shape[1:]
    for c in tiles(chans):
        for i in range(3):
            here = da_ref[i, :, c]
            x = jnp.concatenate([here, rim_ref[i, :, c]], axis=0)
            out_ref[i, :, c] = tap_sum(sm_ref, taps_ref[i, :, c], here, x, rows).astype(BF)


def shares_kernel(keep_ref, recv_ref, own_ref, *share_refs):
    count = len(share_refs) + 1
    shard = own_ref.shape[0] - FEAT_ROWS
    taps = keep_ref.shape[0] - FEAT_ROWS
    feat = (keep_ref[taps:, :] + recv_ref[taps:, :].astype(F32)).astype(BF)
    for d in range(count):
        at = pl.ds(pl.multiple_of(lax.rem(lax.axis_index("ctx") + d, count) * shard, 8), shard)
        total = keep_ref[at, :] + recv_ref[at, :].astype(F32)
        ref = own_ref if d == 0 else share_refs[d - 1]
        ref[:shard, :] = total.astype(ref.dtype)
        ref[shard:, :] = feat.astype(ref.dtype)


def finish_kernel(own_ref, *refs):
    shares, (out_ref, slot_ref) = refs[:-2], refs[-2:]
    count = len(shares) + 1
    shard = own_ref.shape[0] - FEAT_ROWS
    total = own_ref[:shard, :]
    for share in shares:
        total = total + share[:shard, :].astype(F32)
    out_ref[:shard, :] = total
    for d, share in enumerate((own_ref, *shares)):
        slot_ref[lax.rem(lax.axis_index("ctx") + (count - d), count)] = share[shard:, :].astype(F32)
    total = slot_ref[0]
    for d in range(1, count):
        total = total + slot_ref[d]
    out_ref[shard:, :] = total


def joined_kernel(mine_ref, other_ref, dfilt_ref, dfeat_ref):
    shard, width = dfilt_ref.shape[0], mine_ref.shape[1]
    here = pl.multiple_of(lax.axis_index("sub") * width, 128)
    there = pl.multiple_of((1 - lax.axis_index("sub")) * width, 128)
    for at, half in ((here, mine_ref), (there, other_ref)):
        dfilt_ref[:, pl.ds(at, width)] = half[:shard, :]
        for i in range(3):
            dfeat_ref[i, :, pl.ds(at, width)] = half[shard + 8 * i : shard + 8 * i + KF, :]


def local(streams, feat_taps, long_filter, upstream, score_dir, seg_lengths, list_ids):
    rows, chans = streams.shape[1:]
    segs = seg_lengths.shape[0]
    shard = long_filter.shape[0]
    ring = ("ctx", "sub")
    tokens = rows * lax.axis_size("ctx") * lax.axis_size("sub")
    shards = lax.axis_size("ctx")
    ahead, behind, own_wave, back = half_wave(rows)
    after, before = ahead[:, rows:], behind[:, rows:]
    ahead, own_wave, back, after, before = (jnp.asarray(t) for t in (ahead, own_wave, back, after, before))
    direction = score_dir.reshape(1, chans)

    smem = pl.BlockSpec(memory_space=pltpu.SMEM)
    anywhere = pl.BlockSpec(memory_space=pl.ANY)
    here = pl.BlockSpec(memory_space=pltpu.VMEM)
    out = lambda dtype, *shape: jax.ShapeDtypeStruct(shape, dtype)
    vmem = lambda dtype, *shape: pltpu.VMEM(shape, dtype)
    def call(kernel, name, us, scalars, arrays, outs, scratch, **more):
        return pl.pallas_call(
            lambda *refs: kernel(*((tokens,) if scalars else ()), *refs),
            in_specs=[smem] * len(scalars) + [here] * len(arrays),
            out_specs=jax.tree.map(lambda _: here, outs), out_shape=outs, scratch_shapes=scratch,
            compiler_params=pltpu.CompilerParams(vmem_limit_bytes=VMEM_LIMIT),
            cost_estimate=pl.CostEstimate(flops=int(us * 1e7), bytes_accessed=int(us * 3e4), transcendentals=0),
            name=name, **more,
        )(*scalars, *arrays)

    in_hbm = pl.BlockSpec(memory_space=pltpu.HBM)
    shifts = out(BF, (KF - 1) * rows, rows + RIM)
    table = lambda *shape: out(jnp.int32, *shape)
    (sq, tails, part, streams, feat_taps, upstream, own_shifts, next_shifts, back_shifts,
     seg_ahead, seg_before, seg_rows) = pl.pallas_call(
        lambda *refs: cut_kernel(tokens, *refs),
        in_specs=[in_hbm] * 5, out_specs=[here] * 12,
        out_shape=[out(BF, rows, chans), out(BF, 3, RIM, chans), out(BF, shard, chans // 2),
                   out(BF, *streams.shape), out(F32, *feat_taps.shape), out(BF, *upstream.shape),
                   shifts, shifts, shifts, table(2 * rows, 2 * rows), table(2 * rows, rows), table(rows, 2 * rows)],
        scratch_shapes=[pltpu.SMEM((segs,), jnp.int32), pltpu.SemaphoreType.DMA((7,))],
        compiler_params=pltpu.CompilerParams(vmem_limit_bytes=VMEM_LIMIT), name="cut",
    )(*(pltpu.with_memory_space_constraint(x, pltpu.HBM)
        for x in (streams, long_filter, feat_taps, upstream, seg_lengths)))
    held, order = part[None], [0]
    distance = shards // 2
    if distance:
        held = jnp.concatenate([held, swapped(held, "ctx", distance)], axis=0)
        order = [0, distance]
    halo = passed_along(tails, ring, 1)
    held, halo, sq = lax.optimization_barrier((held, halo, sq))
    sq_next = passed_along(sq, ring, -1)
    distance //= 2
    while distance:
        held = jnp.concatenate([held, swapped(held, "ctx", distance)], axis=0)
        order = order + [n ^ distance for n in order]
        distance //= 2
    mine = jnp.stack([held[order.index(n)] for n in range(shards)])

    query, key_feat, value_feat, product, moved = call(
        feat_kernel, "feats", 4, [], [streams, halo, feat_taps, own_shifts],
        [out(BF, rows, chans)] * 4 + [out(BF, KEPT, (KF - 1) * rows, chans)], [])
    z_prev = passed_along(product, ring, 1)
    one_spectrum, one_product = vmem(F32, 2 * rows, chans), vmem(BF, 2 * rows, chans)
    spectra = out(BF, segs, 2 * rows, chans)
    z_spec, q_spec, cross = call(
        spectra_kernel, "own_spectra", 4, [seg_lengths], [product, query, own_wave, seg_ahead],
        [spectra] * 3, [one_spectrum, one_spectrum])

    mine, z_spec = lax.optimization_barrier((mine, z_spec))
    other = swapped(mine, "sub", 1)

    q_next, qn_spec, spectrum, rim_cross, partial = call(
        score_kernel, "scores", 4, [seg_lengths],
        [streams, sq_next, feat_taps, mine, other, direction, z_spec, cross, after, own_wave, next_shifts, seg_ahead],
        [out(BF, rows, chans), out(BF, 2 * rows, chans), out(F32, 2 * rows, chans), out(BF, 2 * rows, chans),
         out(F32, segs, 128)],
        [vmem(F32, LH, chans), one_spectrum])
    up_held, partial = lax.optimization_barrier((upstream, partial))
    up_next = passed_along(up_held, ring, -1)

    def mixed_of(z_spec):
        return call(w_kernel, "mixed", 4, [seg_lengths], [z_spec, z_prev, spectrum, before, back, seg_before, seg_rows],
                    out(F32, rows, chans), [one_product, one_spectrum])

    def u_of(z_spec):
        return call(u_kernel, "spectra_of_up", 4, [seg_lengths],
                    [query, q_next, upstream, up_next, z_spec, ahead, seg_ahead],
                    [spectra, out(F32, 2 * rows, chans)], [one_product, one_spectrum], input_output_aliases={5: 0})

    totals = partial
    mixed = None
    steps = [(axis, 1 << n) for axis in ("sub", "fsdp", "ctx") for n in range(lax.axis_size(axis).bit_length() - 1)]
    for n, (axis, distance) in enumerate(steps):
        arrived = swapped(totals, axis, distance)
        if n == 1:
            mixed = mixed_of(z_spec)
            arrived, mixed, z_spec = lax.optimization_barrier((arrived, mixed, z_spec))
        if n == len(steps) - 1:
            u_spec, a_total = u_of(z_spec)
            arrived, u_spec = lax.optimization_barrier((arrived, u_spec))
        totals = totals + arrived

    grads, heads, coef = call(
        grads_kernel, "gradients", 2, [seg_lengths, list_ids],
        [totals, query, key_feat, value_feat, upstream, direction, mixed, spectrum, u_spec, q_spec, qn_spec, back, seg_rows],
        [out(BF, 3, rows, chans), out(BF, 3, RIM, chans), out(F32, segs, 128)],
        [vmem(F32, rows, 128), vmem(F32, rows, chans), one_product])
    rim = passed_along(heads, ring, -1)
    def weights_of(mine, dtype, grads):
        return call(lambda tokens, *refs: weights_kernel(tokens, mine, *refs), "weight_grads", 2, [seg_lengths],
                    [coef, streams, halo, moved, grads, direction, a_total, rim_cross, cross, back, own_shifts],
                    out(dtype, LH + FEAT_ROWS, chans // 2), [vmem(F32, 2 * rows, chans // 2)])

    send = weights_of(False, BF, grads)
    received = swapped(send, "sub", 1)
    grads, send = lax.optimization_barrier((grads, send))
    keep = weights_of(True, F32, grads)
    keep, rim = lax.optimization_barrier((keep, rim))
    shares = call(
        shares_kernel, "shares", 1, [], [keep, received],
        [out(F32, shard + FEAT_ROWS, chans // 2)] + [out(BF, shard + FEAT_ROWS, chans // 2)] * (shards - 1), [])
    parts = [rotated(shares[d], "ctx", d) for d in range(1, shards)]
    d_streams = call(
        dstreams_kernel, "stream_grads", 4, [], [grads, rim, feat_taps, back_shifts], out(BF, 3, rows, chans), [])
    parts, d_streams = lax.optimization_barrier((parts, d_streams))
    summed = call(
        finish_kernel, "shard_sums", 1, [], [shares[0], *parts], out(F32, shard + FEAT_ROWS, chans // 2),
        [vmem(F32, shards, FEAT_ROWS, chans // 2)])
    d_filter, d_feat = call(
        joined_kernel, "both_halves", 1, [], [summed, swapped(summed, "sub", 1)],
        [out(F32, shard, chans), out(F32, 3, KF, chans)], [])
    return (d_streams, d_feat, d_filter)


def solution(mesh):
    placed = (
        P(None, ("groups", "ctx", "sub"), "fsdp"),
        P(None, None, "fsdp"),
        P("ctx", "fsdp"),
        P(("groups", "ctx", "sub"), "fsdp"),
        P("fsdp"),
        P("groups"),
        P("groups"),
    )
    return jax.shard_map(
        local,
        mesh=mesh,
        in_specs=placed,
        out_specs=(
            P(None, ("groups", "ctx", "sub"), "fsdp"),
            P("groups", None, "fsdp"),
            P(("groups", "ctx"), "fsdp"),
        ),
        check_vma=False,
    )
```
